512 devices in a mesh: vel: 64 (over x, y, z_lo), cell: 8 (over z_hi, core).
Axes of the slice: x: 4, y: 8, z: 8 (z_hi: 4, z_lo: 2; z = z_hi * 2 + z_lo), core: 2. Of those that a mesh axis runs over, the one named last changes fastest.
Arguments:
- state_init: float32 [13824, 16, 1024], P('vel', 'cell'), as said below
- cell_kind: int32 [16, 1024], P('cell'), may hold values from 0 to 3, as said below
- boundary_state: float32 [6], replicated, may hold values from 0.5 to 1.5
Outputs:
- state_final: float32 [13824, 16, 1024], P('vel', 'cell')
- macro: float32 [5, 16, 1024], P(None, 'cell')
The draws below stay inside these ranges and needn't reach their ends.
Inputs may be any that keep to these rules, and one draw needn't show every extreme that they name: `state_init`: positive everywhere. `cell_kind`: the first cell plane along the nozzle axis holds only inlet and wall cells, the last plane only outlet cells.
All inputs are finite; a program needn't handle non-finite values.
Results may differ from the reference program's by a relative error of at most 0.0003.
Values sent between devices are 32-bit elements; how exact they have to be, the bound alone decides.
A program may use at most 128 MiB of HBM per device.

```python
import jax
import jax.numpy as jnp
import numpy as np
from jax import lax

QUAD_ABSCISSAE = 24
NY = 32
NZ = 32
STEPS = 2
NOZZLE_LAYERS = 16


def hermite_rule_drawn(points):
    start_value = np.pi ** (-0.25)
    node_list = np.zeros(points)
    weight_list = np.zeros(points)
    guess_root = 0.0
    slope_value = 1.0
    for index in range((points + 1) // 2):
        if index == 0:
            guess_root = np.sqrt(2.0 * points + 1.0) - 1.85575 * (2.0 * points + 1.0) ** (-0.16667)
        elif index == 1:
            guess_root = guess_root - 1.14 * points ** 0.426 / guess_root
        elif index == 2:
            guess_root = 1.86 * guess_root - 0.86 * node_list[0]
        elif index == 3:
            guess_root = 1.91 * guess_root - 0.91 * node_list[1]
        else:
            guess_root = 2.0 * guess_root - node_list[index - 2]
        for sweep in range(60):
            poly_now = start_value
            poly_prev = 0.0
            for degree in range(points):
                poly_old = poly_prev
                poly_prev = poly_now
                poly_now = guess_root * np.sqrt(2.0 / (degree + 1)) * poly_prev - np.sqrt(degree / (degree + 1.0)) * poly_old
            slope_value = np.sqrt(2.0 * points) * poly_prev
            guess_root = guess_root - poly_now / slope_value
        node_list[index] = guess_root
        node_list[points - 1 - index] = -guess_root
        weight_list[index] = 2.0 / (slope_value * slope_value)
        weight_list[points - 1 - index] = weight_list[index]
    return node_list[::-1].copy()


def draw_state_init(key, part):
    abscissa = hermite_rule_drawn(QUAD_ABSCISSAE)
    one_dimensional_abscissae = jnp.asarray(np.sqrt(2.0) * abscissa, jnp.float32)
    mixed_products = NY * NZ
    stride = QUAD_ABSCISSAE // 4
    key_a, another_random_seed, key_c, key_d = jax.random.split(key, 4)
    particle_concentration = jnp.exp(jax.random.uniform(key_a, (NOZZLE_LAYERS, mixed_products), jnp.float32, np.log(0.3), np.log(3.0)))
    thermal_level = jnp.exp(jax.random.uniform(another_random_seed, (NOZZLE_LAYERS, mixed_products), jnp.float32, np.log(0.1), np.log(2.0)))
    mean_flow_vector = 0.5 * jnp.clip(jax.random.normal(key_c, (3, NOZZLE_LAYERS, mixed_products), jnp.float32), -2.5, 2.5)
    noise = jax.random.uniform(key_d, (QUAD_ABSCISSAE ** 3, NOZZLE_LAYERS, mixed_products), jnp.float32, 0.7, 1.3)
    correction_multipliers = [jnp.exp(-(one_dimensional_abscissae[:, None, None] - mean_flow_vector[coordinate_choice]) ** 2 / (2.0 * thermal_level)) for coordinate_choice in range(3)]
    reordered = [factor.reshape(stride, 4, NOZZLE_LAYERS, mixed_products).transpose(1, 0, 2, 3) for factor in correction_multipliers]
    full_extent_layout = reordered[0][:, None, None, :, None, None] * reordered[1][None, :, None, None, :, None] * reordered[2][None, None, :, None, None, :]
    particle_population = particle_concentration * thermal_level ** (-1.5) * full_extent_layout.reshape(QUAD_ABSCISSAE ** 3, NOZZLE_LAYERS, mixed_products)
    return (particle_population * noise).astype(jnp.float32)


def draw_cell_kind(key, part):
    mixed_products = NY * NZ
    key_a, another_random_seed = jax.random.split(key)
    radius = jax.random.randint(key_a, (), max(min(NY, NZ) // 4, 1), min(NY, NZ) // 2 + 1)
    flat = lax.broadcasted_iota(jnp.int32, (NOZZLE_LAYERS, mixed_products), 1)
    plane = lax.broadcasted_iota(jnp.int32, (NOZZLE_LAYERS, mixed_products), 0)
    y_pos = flat // NZ
    z_pos = flat % NZ
    dist = (2 * y_pos + 1 - NY) ** 2 + (2 * z_pos + 1 - NZ) ** 2
    inlet = dist <= 4 * radius * radius
    lips = jax.random.randint(another_random_seed, (NOZZLE_LAYERS, mixed_products), 0, 100) < 6
    kinds = jnp.where(lips, 1, 0)
    kinds = jnp.where(plane == 0, jnp.where(inlet, 2, 1), kinds)
    kinds = jnp.where(plane == NOZZLE_LAYERS - 1, 3, kinds)
    return kinds.astype(jnp.int32)


def setup_inputs(seed: int = 0) -> dict:
    arg_keys = jax.random.split(jax.random.key(seed), 4)
    return {
        "state_init": draw_state_init(jax.random.fold_in(arg_keys[3], 71), 0),
        "cell_kind": draw_cell_kind(jax.random.fold_in(arg_keys[3], 71), 0),
        "boundary_state": jnp.clip(jax.random.uniform(arg_keys[2], (6,), jnp.float32, 0.5, 1.5), 0.5, 1.5),
    }


MOMENTUM_RATIO = 2.0 / 3.0
SHEAR_EXPONENT = 0.81
SHEAR_REFERENCE = 0.05
TIME_INCREMENT = 0.03125

def hermite_rule(points):
    start_value = np.pi ** (-0.25)
    node_list = np.zeros(points)
    weight_list = np.zeros(points)
    guess_root = 0.0
    slope_value = 1.0
    for index in range((points + 1) // 2):
        if index == 0:
            guess_root = np.sqrt(2.0 * points + 1.0) - 1.85575 * (2.0 * points + 1.0) ** (-0.16667)
        elif index == 1:
            guess_root = guess_root - 1.14 * points ** 0.426 / guess_root
        elif index == 2:
            guess_root = 1.86 * guess_root - 0.86 * node_list[0]
        elif index == 3:
            guess_root = 1.91 * guess_root - 0.91 * node_list[1]
        else:
            guess_root = 2.0 * guess_root - node_list[index - 2]
        for sweep in range(60):
            poly_now = start_value
            poly_prev = 0.0
            for degree in range(points):
                poly_old = poly_prev
                poly_prev = poly_now
                poly_now = guess_root * np.sqrt(2.0 / (degree + 1)) * poly_prev - np.sqrt(degree / (degree + 1.0)) * poly_old
            slope_value = np.sqrt(2.0 * points) * poly_prev
            guess_root = guess_root - poly_now / slope_value
        node_list[index] = guess_root
        node_list[points - 1 - index] = -guess_root
        weight_list[index] = 2.0 / (slope_value * slope_value)
        weight_list[points - 1 - index] = weight_list[index]
    return (node_list[::-1].copy(), weight_list[::-1].copy())

def node_order(points):
    stride = points // 4
    pieces = np.meshgrid(np.arange(4), np.arange(4), np.arange(4), np.arange(stride), np.arange(stride), np.arange(stride), indexing='ij')
    return [(4 * pieces[3 + axis_number] + pieces[axis_number]).reshape(-1) for axis_number in range(3)]

def node_table(points):
    abscissa, weights = hermite_rule(points)
    one_dimensional_abscissae = np.sqrt(2.0) * abscissa
    weights_one = weights * np.exp(abscissa * abscissa) / np.sqrt(np.pi)
    order_a, order_b, order_c = node_order(points)
    speeds = np.stack([one_dimensional_abscissae[order_a], one_dimensional_abscissae[order_b], one_dimensional_abscissae[order_c]])
    quadrature = weights_one[order_a] * weights_one[order_b] * weights_one[order_c]
    return (speeds, quadrature)

def moment_rows(speeds, quadrature):
    speed_x, speed_y, speed_z = (speeds[0], speeds[1], speeds[2])
    square = speed_x * speed_x + speed_y * speed_y + speed_z * speed_z
    return np.stack([quadrature, quadrature * speed_x, quadrature * speed_y, quadrature * speed_z, quadrature * speed_x * speed_x, quadrature * speed_y * speed_y, quadrature * speed_z * speed_z, quadrature * speed_x * speed_y, quadrature * speed_x * speed_z, quadrature * speed_y * speed_z, quadrature * speed_x * square, quadrature * speed_y * square, quadrature * speed_z * square])

def equilibrium_fields(moments):
    particle_concentration = moments[0]
    first = (moments[1], moments[2], moments[3])
    mean_flow_vector = (first[0] / particle_concentration, first[1] / particle_concentration, first[2] / particle_concentration)
    diagonal_tensor_total = moments[4] + moments[5] + moments[6]
    lattice_magnitude_squared = mean_flow_vector[0] * mean_flow_vector[0] + mean_flow_vector[1] * mean_flow_vector[1] + mean_flow_vector[2] * mean_flow_vector[2]
    thermal_level = (diagonal_tensor_total / particle_concentration - lattice_magnitude_squared) / 3.0
    pairs = ((4, 7, 8), (7, 5, 9), (8, 9, 6))
    along = mean_flow_vector[0] * first[0] + mean_flow_vector[1] * first[1] + mean_flow_vector[2] * first[2]
    energy_current_vectors = []
    for coordinate_choice in range(3):
        tensor_part = moments[pairs[coordinate_choice][0]] * mean_flow_vector[0] + moments[pairs[coordinate_choice][1]] * mean_flow_vector[1] + moments[pairs[coordinate_choice][2]] * mean_flow_vector[2]
        energy_current_vectors.append(0.5 * (moments[10 + coordinate_choice] - 2.0 * tensor_part + lattice_magnitude_squared * first[coordinate_choice] - mean_flow_vector[coordinate_choice] * diagonal_tensor_total + 2.0 * mean_flow_vector[coordinate_choice] * along - mean_flow_vector[coordinate_choice] * lattice_magnitude_squared * particle_concentration))
    return jnp.stack([particle_concentration, mean_flow_vector[0], mean_flow_vector[1], mean_flow_vector[2], thermal_level, energy_current_vectors[0], energy_current_vectors[1], energy_current_vectors[2]])

def transport(padded, speeds, depth_z):
    center = padded[:, 1:-1]
    speed_x = speeds[0][:, None, None]
    speed_y = speeds[1][:, None, None]
    speed_z = speeds[2][:, None, None]
    grad_x = jnp.where(speed_x > 0, center - padded[:, :-2], padded[:, 2:] - center)
    mixed_products = center.shape[2]
    zeros_one = jnp.zeros(center.shape[:2] + (1,), center.dtype)
    zeros_row = jnp.zeros(center.shape[:2] + (depth_z,), center.dtype)
    z_index = lax.broadcasted_iota(jnp.int32, (1, 1, mixed_products), 2) % depth_z
    below_z = jnp.where(z_index == 0, 0.0, jnp.concatenate([zeros_one, center[..., :-1]], 2))
    above_z = jnp.where(z_index == depth_z - 1, 0.0, jnp.concatenate([center[..., 1:], zeros_one], 2))
    below_y = jnp.concatenate([zeros_row, center[..., :-depth_z]], 2)
    above_y = jnp.concatenate([center[..., depth_z:], zeros_row], 2)
    grad_y = jnp.where(speed_y > 0, center - below_y, above_y - center)
    grad_z = jnp.where(speed_z > 0, center - below_z, above_z - center)
    return center - TIME_INCREMENT * (speed_x * grad_x + speed_y * grad_y + speed_z * grad_z)

def relax(moved, moment_quantities, kinds, speeds, boundary):
    particle_concentration, thermal_level = (moment_quantities[0], moment_quantities[4])
    mean_flow_vector = (moment_quantities[1], moment_quantities[2], moment_quantities[3])
    heat = (moment_quantities[5], moment_quantities[6], moment_quantities[7])
    comps = [speeds[coordinate_choice][:, None, None] - mean_flow_vector[coordinate_choice] for coordinate_choice in range(3)]
    relative_magnitude_squared = comps[0] * comps[0] + comps[1] * comps[1] + comps[2] * comps[2]
    isotropic_load = particle_concentration * thermal_level
    equilibrium_profile = particle_concentration * thermal_level ** (-1.5) * jnp.exp(-relative_magnitude_squared / (2.0 * thermal_level))
    energy_current_projection = comps[0] * heat[0] + comps[1] * heat[1] + comps[2] * heat[2]
    corrected_equilibrium = equilibrium_profile * (1.0 + (1.0 - MOMENTUM_RATIO) * energy_current_projection * (relative_magnitude_squared / thermal_level - 5.0) / (5.0 * isotropic_load * thermal_level))
    relaxation_frequency = TIME_INCREMENT * isotropic_load / (SHEAR_REFERENCE * thermal_level ** SHEAR_EXPONENT)
    relaxed = (moved + relaxation_frequency * corrected_equilibrium) / (1.0 + relaxation_frequency)
    node_sq = (speeds[0] * speeds[0] + speeds[1] * speeds[1] + speeds[2] * speeds[2])[:, None, None]
    wall_temp = boundary[5]
    wall = particle_concentration * wall_temp ** (-1.5) * jnp.exp(-node_sq / (2.0 * wall_temp))
    inlet_sq = ((speeds[0] - boundary[1]) ** 2 + (speeds[1] - boundary[2]) ** 2 + (speeds[2] - boundary[3]) ** 2)[:, None, None]
    inlet = boundary[0] * boundary[4] ** (-1.5) * jnp.exp(-inlet_sq / (2.0 * boundary[4]))
    return jnp.where(kinds == 0, relaxed, jnp.where(kinds == 1, wall, jnp.where(kinds == 2, inlet, moved)))

def reference(state_init, cell_kind, boundary_state):
    speeds_np, quadrature = node_table(QUAD_ABSCISSAE)
    speeds = jnp.asarray(speeds_np, jnp.float32)
    weights = jnp.asarray(moment_rows(speeds_np, quadrature), jnp.float32)
    block = QUAD_ABSCISSAE * QUAD_ABSCISSAE
    mixed_products = NY * NZ
    block_ids = jnp.arange(QUAD_ABSCISSAE, dtype=jnp.int32)

    def moved_block(particle_population, block_index):
        start = (block_index * block).astype(jnp.int32)
        piece = lax.dynamic_slice_in_dim(particle_population, start, block, 0)
        block_speeds = lax.dynamic_slice_in_dim(speeds, start, block, 1)
        padded = jnp.pad(piece, ((0, 0), (1, 1), (0, 0)))
        return (transport(padded, block_speeds, NZ), block_speeds, start)

    def moments_of(particle_population, with_transport):

        def accumulate(total, block_index):
            if with_transport:
                moved, block_speeds, start = moved_block(particle_population, block_index)
            else:
                start = (block_index * block).astype(jnp.int32)
                moved = lax.dynamic_slice_in_dim(particle_population, start, block, 0)
            block_rows = lax.dynamic_slice_in_dim(weights, start, block, 1)
            return (total + jnp.dot(block_rows, moved.reshape(block, NOZZLE_LAYERS * mixed_products), precision=lax.Precision.HIGHEST), None)
        total, unused = lax.scan(accumulate, jnp.zeros((13, NOZZLE_LAYERS * mixed_products), jnp.float32), block_ids)
        return total
    particle_population = state_init
    for section in range(STEPS):
        moment_quantities = equilibrium_fields(moments_of(particle_population, True)).reshape(8, NOZZLE_LAYERS, mixed_products)

        def advance(block_index):
            moved, block_speeds, start = moved_block(particle_population, block_index)
            return relax(moved, moment_quantities, cell_kind, block_speeds, boundary_state)
        particle_population = lax.map(advance, block_ids).reshape(QUAD_ABSCISSAE * block, NOZZLE_LAYERS, mixed_products)
    final = equilibrium_fields(moments_of(particle_population, False)).reshape(8, NOZZLE_LAYERS, mixed_products)
    return (particle_population, final[:5])
```

```python
import jax
import jax.numpy as jnp
import numpy as np
from jax import lax
from jax.experimental import pallas as pl
from jax.experimental.pallas import tpu as pltpu
from jax.sharding import PartitionSpec as P

QUAD_ABSCISSAE = 24
NZ = 32
STEPS = 2


MOMENTUM_RATIO = 2.0 / 3.0
SHEAR_EXPONENT = 0.81
SHEAR_REFERENCE = 0.05
TIME_INCREMENT = 0.03125


def extended(cells, sides, width):
    for axis, dim in sides:
        count = lax.axis_size(axis)
        ends = count - 1
        head = lax.slice_in_dim(cells, 0, width, axis=dim)
        tail = lax.slice_in_dim(cells, cells.shape[dim] - width, cells.shape[dim], axis=dim)
        cells = jnp.concatenate(
            [
                lax.ppermute(tail, axis, [(i, (i + 1) % count) for i in range(ends)]),
                cells,
                lax.ppermute(head, axis, [((i + 1) % count, i) for i in range(ends)]),
            ],
            axis=dim,
        )
    return cells


def hermite_rule(points):
    start_value = np.pi ** (-0.25)
    node_list = np.zeros(points)
    weight_list = np.zeros(points)
    guess_root = 0.0
    slope_value = 1.0
    for index in range((points + 1) // 2):
        if index == 0:
            guess_root = np.sqrt(2.0 * points + 1.0) - 1.85575 * (2.0 * points + 1.0) ** (-0.16667)
        elif index == 1:
            guess_root = guess_root - 1.14 * points**0.426 / guess_root
        elif index == 2:
            guess_root = 1.86 * guess_root - 0.86 * node_list[0]
        elif index == 3:
            guess_root = 1.91 * guess_root - 0.91 * node_list[1]
        else:
            guess_root = 2.0 * guess_root - node_list[index - 2]
        for sweep in range(60):
            poly_now = start_value
            poly_prev = 0.0
            for degree in range(points):
                poly_old = poly_prev
                poly_prev = poly_now
                poly_now = (
                    guess_root * np.sqrt(2.0 / (degree + 1)) * poly_prev
                    - np.sqrt(degree / (degree + 1.0)) * poly_old
                )
            slope_value = np.sqrt(2.0 * points) * poly_prev
            guess_root = guess_root - poly_now / slope_value
        node_list[index] = guess_root
        node_list[points - 1 - index] = -guess_root
        weight_list[index] = 2.0 / (slope_value * slope_value)
        weight_list[points - 1 - index] = weight_list[index]
    return (node_list[::-1].copy(), weight_list[::-1].copy())


def node_order(points):
    stride = points // 4
    pieces = np.meshgrid(
        np.arange(4),
        np.arange(4),
        np.arange(4),
        np.arange(stride),
        np.arange(stride),
        np.arange(stride),
        indexing="ij",
    )
    return [
        (4 * pieces[3 + axis_number] + pieces[axis_number]).reshape(-1) for axis_number in range(3)
    ]


def node_table(points):
    abscissa, weights = hermite_rule(points)
    one_dimensional_abscissae = np.sqrt(2.0) * abscissa
    weights_one = weights * np.exp(abscissa * abscissa) / np.sqrt(np.pi)
    order_a, order_b, order_c = node_order(points)
    speeds = np.stack(
        [
            one_dimensional_abscissae[order_a],
            one_dimensional_abscissae[order_b],
            one_dimensional_abscissae[order_c],
        ]
    )
    quadrature = weights_one[order_a] * weights_one[order_b] * weights_one[order_c]
    return (speeds, quadrature)


def moment_rows(speeds, quadrature):
    speed_x, speed_y, speed_z = (speeds[0], speeds[1], speeds[2])
    square = speed_x * speed_x + speed_y * speed_y + speed_z * speed_z
    return np.stack(
        [
            quadrature,
            quadrature * speed_x,
            quadrature * speed_y,
            quadrature * speed_z,
            quadrature * speed_x * speed_x,
            quadrature * speed_y * speed_y,
            quadrature * speed_z * speed_z,
            quadrature * speed_x * speed_y,
            quadrature * speed_x * speed_z,
            quadrature * speed_y * speed_z,
            quadrature * speed_x * square,
            quadrature * speed_y * square,
            quadrature * speed_z * square,
        ]
    )


def equilibrium_fields(moments):
    particle_concentration = moments[0]
    first = (moments[1], moments[2], moments[3])
    mean_flow_vector = (
        first[0] / particle_concentration,
        first[1] / particle_concentration,
        first[2] / particle_concentration,
    )
    diagonal_tensor_total = moments[4] + moments[5] + moments[6]
    lattice_magnitude_squared = (
        mean_flow_vector[0] * mean_flow_vector[0]
        + mean_flow_vector[1] * mean_flow_vector[1]
        + mean_flow_vector[2] * mean_flow_vector[2]
    )
    thermal_level = (
        diagonal_tensor_total / particle_concentration - lattice_magnitude_squared
    ) / 3.0
    pairs = ((4, 7, 8), (7, 5, 9), (8, 9, 6))
    along = (
        mean_flow_vector[0] * first[0]
        + mean_flow_vector[1] * first[1]
        + mean_flow_vector[2] * first[2]
    )
    energy_current_vectors = []
    for coordinate_choice in range(3):
        tensor_part = (
            moments[pairs[coordinate_choice][0]] * mean_flow_vector[0]
            + moments[pairs[coordinate_choice][1]] * mean_flow_vector[1]
            + moments[pairs[coordinate_choice][2]] * mean_flow_vector[2]
        )
        energy_current_vectors.append(
            0.5
            * (
                moments[10 + coordinate_choice]
                - 2.0 * tensor_part
                + lattice_magnitude_squared * first[coordinate_choice]
                - mean_flow_vector[coordinate_choice] * diagonal_tensor_total
                + 2.0 * mean_flow_vector[coordinate_choice] * along
                - mean_flow_vector[coordinate_choice]
                * lattice_magnitude_squared
                * particle_concentration
            )
        )
    return jnp.stack(
        [
            particle_concentration,
            mean_flow_vector[0],
            mean_flow_vector[1],
            mean_flow_vector[2],
            thermal_level,
            energy_current_vectors[0],
            energy_current_vectors[1],
            energy_current_vectors[2],
        ]
    )


def transport(padded, speeds, depth_z):
    center = padded[:, 1:-1]
    speed_x = speeds[0][:, None, None]
    speed_y = speeds[1][:, None, None]
    speed_z = speeds[2][:, None, None]
    grad_x = jnp.where(speed_x > 0, center - padded[:, :-2], padded[:, 2:] - center)
    mixed_products = center.shape[2]
    zeros_one = jnp.zeros(center.shape[:2] + (1,), center.dtype)
    zeros_row = jnp.zeros(center.shape[:2] + (depth_z,), center.dtype)
    z_index = lax.broadcasted_iota(jnp.int32, (1, 1, mixed_products), 2) % depth_z
    below_z = jnp.where(z_index == 0, 0.0, jnp.concatenate([zeros_one, center[..., :-1]], 2))
    above_z = jnp.where(
        z_index == depth_z - 1, 0.0, jnp.concatenate([center[..., 1:], zeros_one], 2)
    )
    below_y = jnp.concatenate([zeros_row, center[..., :-depth_z]], 2)
    above_y = jnp.concatenate([center[..., depth_z:], zeros_row], 2)
    grad_y = jnp.where(speed_y > 0, center - below_y, above_y - center)
    grad_z = jnp.where(speed_z > 0, center - below_z, above_z - center)
    return center - TIME_INCREMENT * (speed_x * grad_x + speed_y * grad_y + speed_z * grad_z)


def relax(moved, moment_quantities, kinds, speeds, boundary):
    particle_concentration, thermal_level = (moment_quantities[0], moment_quantities[4])
    mean_flow_vector = (moment_quantities[1], moment_quantities[2], moment_quantities[3])
    heat = (moment_quantities[5], moment_quantities[6], moment_quantities[7])
    comps = [
        speeds[coordinate_choice][:, None, None] - mean_flow_vector[coordinate_choice]
        for coordinate_choice in range(3)
    ]
    relative_magnitude_squared = comps[0] * comps[0] + comps[1] * comps[1] + comps[2] * comps[2]
    isotropic_load = particle_concentration * thermal_level
    equilibrium_profile = (
        particle_concentration
        * thermal_level ** (-1.5)
        * jnp.exp(-relative_magnitude_squared / (2.0 * thermal_level))
    )
    energy_current_projection = comps[0] * heat[0] + comps[1] * heat[1] + comps[2] * heat[2]
    corrected_equilibrium = equilibrium_profile * (
        1.0
        + (1.0 - MOMENTUM_RATIO)
        * energy_current_projection
        * (relative_magnitude_squared / thermal_level - 5.0)
        / (5.0 * isotropic_load * thermal_level)
    )
    relaxation_frequency = (
        TIME_INCREMENT * isotropic_load / (SHEAR_REFERENCE * thermal_level**SHEAR_EXPONENT)
    )
    relaxed = (moved + relaxation_frequency * corrected_equilibrium) / (1.0 + relaxation_frequency)
    node_sq = (speeds[0] * speeds[0] + speeds[1] * speeds[1] + speeds[2] * speeds[2])[:, None, None]
    wall_temp = boundary[5]
    wall = particle_concentration * wall_temp ** (-1.5) * jnp.exp(-node_sq / (2.0 * wall_temp))
    inlet_sq = (
        (speeds[0] - boundary[1]) ** 2
        + (speeds[1] - boundary[2]) ** 2
        + (speeds[2] - boundary[3]) ** 2
    )[:, None, None]
    inlet = boundary[0] * boundary[4] ** (-1.5) * jnp.exp(-inlet_sq / (2.0 * boundary[4]))
    return jnp.where(
        kinds == 0, relaxed, jnp.where(kinds == 1, wall, jnp.where(kinds == 2, inlet, moved))
    )


MESH = pl.DeviceIdType.MESH


def sum_kernel(part_ref, out_ref, got_a, mine, got_b, send_sem, recv_sem):
    vel = lax.axis_index("vel")
    cell = lax.axis_index("cell")
    lo = lax.rem(vel, 2)
    row = lax.rem(vel // 2, 8)
    col = vel // 16
    here = col * 2 + lo

    def peer_a(other):
        return ((other // 2) * 16 + row * 2 + lax.rem(other, 2), cell)

    def peer_b(other):
        return (col * 16 + other * 2 + lo, cell)

    barrier = pltpu.get_barrier_semaphore()
    for k in range(1, 8):
        pl.semaphore_signal(barrier, inc=1, device_id=peer_a(lax.rem(here + k, 8)), device_id_type=MESH)
        pl.semaphore_signal(barrier, inc=1, device_id=peer_b(lax.rem(row + k, 8)), device_id_type=MESH)
    pl.semaphore_wait(barrier, 14)

    def exchange(phase, source, target, index, peer):
        copies = []
        for k in range(1, 8):
            other = lax.rem(index + k, 8)
            copy = pltpu.make_async_remote_copy(
                src_ref=source(other),
                dst_ref=target,
                send_sem=send_sem.at[phase, k - 1],
                recv_sem=recv_sem.at[phase, k - 1],
                device_id=peer(other),
                device_id_type=MESH,
            )
            copy.start()
            copies.append(copy)
        return copies

    copies = exchange(0, lambda other: part_ref.at[other], got_a.at[here], here, peer_a)
    got_a[here] = part_ref[here]
    for copy in copies:
        copy.wait()
    total = got_a[0]
    for k in range(1, 8):
        total = total + got_a[k]
    mine[...] = total
    copies = exchange(1, lambda other: mine, got_b.at[row], row, peer_b)
    got_b[row] = total
    for copy in copies:
        copy.wait()
    total = got_b[0]
    for k in range(1, 8):
        total = total + got_b[k]
    out_ref[here] = total
    copies = exchange(2, lambda other: out_ref.at[here], out_ref.at[here], here, peer_a)
    for copy in copies:
        copy.wait()


def summed(moments):
    rows, cells = moments.shape
    parts = jnp.pad(moments, ((0, 16 - rows), (0, 0))).reshape(16, 2, 8, 128)
    parts = parts.transpose(2, 0, 1, 3).reshape(8, 32, 128)
    total = pl.pallas_call(
        sum_kernel,
        out_shape=jax.ShapeDtypeStruct((8, 32, 128), jnp.float32),
        in_specs=[pl.BlockSpec(memory_space=pltpu.VMEM)],
        out_specs=pl.BlockSpec(memory_space=pltpu.VMEM),
        scratch_shapes=[
            pltpu.VMEM((8, 32, 128), jnp.float32),
            pltpu.VMEM((32, 128), jnp.float32),
            pltpu.VMEM((8, 32, 128), jnp.float32),
            pltpu.SemaphoreType.DMA((3, 7)),
            pltpu.SemaphoreType.DMA((3, 7)),
        ],
        compiler_params=pltpu.CompilerParams(collective_id=0, has_side_effects=True),
    )(parts)
    total = total.reshape(8, 16, 2, 128).transpose(1, 2, 0, 3)
    return total.reshape(16, cells)[:rows]


def shards(state_init, cell_kind, boundary_state):
    count = state_init.shape[0]
    mixed_products = state_init.shape[2]
    speeds_np, quadrature = node_table(QUAD_ABSCISSAE)
    first_node = lax.axis_index("vel") * count
    speeds = lax.dynamic_slice_in_dim(jnp.asarray(speeds_np, jnp.float32), first_node, count, 1)
    weights = lax.dynamic_slice_in_dim(
        jnp.asarray(moment_rows(speeds_np, quadrature), jnp.float32), first_node, count, 1
    )

    def cell_fields(moved):
        depth = moved.shape[1]
        moments = jnp.dot(
            weights, moved.reshape(count, depth * mixed_products), precision=lax.Precision.HIGHEST
        )
        moment_quantities = equilibrium_fields(summed(moments))
        return moment_quantities.reshape(8, depth, mixed_products)

    particle_population = state_init
    for section in range(STEPS):
        padded = extended(particle_population, (("cell", 1),), 1)
        moved = transport(padded, speeds, NZ)
        moment_quantities = cell_fields(moved)
        particle_population = relax(moved, moment_quantities, cell_kind, speeds, boundary_state)
    final = cell_fields(particle_population)
    return (particle_population, final[:5])


def solution(mesh):
    in_specs = (P("vel", "cell", None), P("cell", None), P())
    out_specs = (P("vel", "cell", None), P(None, "cell", None))
    return jax.shard_map(shards, mesh=mesh, in_specs=in_specs, out_specs=out_specs, check_vma=False)
```

```python
import functools

import jax
import jax.numpy as jnp
import numpy as np
from jax import lax
from jax.experimental import pallas as pl
from jax.experimental.pallas import tpu as pltpu
from jax.sharding import PartitionSpec as P

QUAD_ABSCISSAE = 24
RUN = 6
STEPS = 2


MOMENTUM_RATIO = 2.0 / 3.0
SHEAR_EXPONENT = 0.81
SHEAR_REFERENCE = 0.05
TIME_INCREMENT = 0.03125

NODES = RUN * RUN * RUN
HALF = NODES // 2
PAIRS = RUN * RUN
ROWS = 32
MESH = pl.DeviceIdType.MESH


def hermite_rule(points):
    start_value = np.pi ** (-0.25)
    node_list = np.zeros(points)
    weight_list = np.zeros(points)
    guess_root = 0.0
    slope_value = 1.0
    for index in range((points + 1) // 2):
        if index == 0:
            guess_root = np.sqrt(2.0 * points + 1.0) - 1.85575 * (2.0 * points + 1.0) ** (-0.16667)
        elif index == 1:
            guess_root = guess_root - 1.14 * points**0.426 / guess_root
        elif index == 2:
            guess_root = 1.86 * guess_root - 0.86 * node_list[0]
        elif index == 3:
            guess_root = 1.91 * guess_root - 0.91 * node_list[1]
        else:
            guess_root = 2.0 * guess_root - node_list[index - 2]
        for sweep in range(60):
            poly_now = start_value
            poly_prev = 0.0
            for degree in range(points):
                poly_old = poly_prev
                poly_prev = poly_now
                poly_now = (
                    guess_root * np.sqrt(2.0 / (degree + 1)) * poly_prev
                    - np.sqrt(degree / (degree + 1.0)) * poly_old
                )
            slope_value = np.sqrt(2.0 * points) * poly_prev
            guess_root = guess_root - poly_now / slope_value
        node_list[index] = guess_root
        node_list[points - 1 - index] = -guess_root
        weight_list[index] = 2.0 / (slope_value * slope_value)
        weight_list[points - 1 - index] = weight_list[index]
    return (node_list[::-1].copy(), weight_list[::-1].copy())


def one_dimensional_tables(points):
    abscissa, weights = hermite_rule(points)
    speed = np.sqrt(2.0) * abscissa
    weight = weights * np.exp(abscissa * abscissa) / np.sqrt(np.pi)
    return np.concatenate([speed, weight, TIME_INCREMENT * np.abs(speed)])


def step_parameters(moment, kind, boundary):
    density = moment[0]
    first = moment[1:4]
    flow = [value / density for value in first]
    trace = moment[4] + moment[5] + moment[6]
    square = flow[0] * flow[0] + flow[1] * flow[1] + flow[2] * flow[2]
    temperature = (trace / density - square) / 3.0
    along = flow[0] * first[0] + flow[1] * first[1] + flow[2] * first[2]
    pairs = ((4, 7, 8), (7, 5, 9), (8, 9, 6))
    heat = []
    for d in range(3):
        tensor = (
            moment[pairs[d][0]] * flow[0]
            + moment[pairs[d][1]] * flow[1]
            + moment[pairs[d][2]] * flow[2]
        )
        heat.append(
            0.5
            * (
                moment[10 + d]
                - 2.0 * tensor
                + square * first[d]
                - flow[d] * trace
                + 2.0 * flow[d] * along
                - flow[d] * square * density
            )
        )
    pressure = density * temperature
    rate = (
        TIME_INCREMENT
        * pressure
        / (SHEAR_REFERENCE * jnp.exp(SHEAR_EXPONENT * jnp.log(temperature)))
    )
    keep = 1.0 / (1.0 + rate)
    scale = (1.0 - MOMENTUM_RATIO) / (5.0 * pressure * temperature)

    def pick(fluid, wall, inlet, outlet):
        return jnp.where(
            kind == 0, fluid, jnp.where(kind == 1, wall, jnp.where(kind == 2, inlet, outlet))
        )

    level = pick(temperature, boundary[5], boundary[4], 1.0)
    amount = pick(density * rate * keep, density, boundary[0], 0.0)
    return (
        [pick(keep, 0.0, 0.0, 1.0), amount / (level * jnp.sqrt(level))]
        + [pick(flow[d], 0.0, boundary[1 + d], 0.0) for d in range(3)]
        + [0.5 / level]
        + [pick(heat[d] * scale, 0.0, 0.0, 0.0) for d in range(3)]
        + [density, first[0], first[1], first[2], trace]
    )


def added_moments(power, amount, flow, inverse, heat):
    planes = {}

    def product(i, j, k):
        if (i, j) not in planes:
            planes[i, j] = power[0][i] * power[1][j]
        return planes[i, j] * power[2][k]

    def shifted(base, d, n=1):
        return tuple(base[e] + (n if e == d else 0) for e in range(3))

    def squared(base):
        return product(*shifted(base, 0, 2)) + product(*shifted(base, 1, 2)) + product(*shifted(base, 2, 2))

    double = inverse + inverse

    def whole(base):
        total = product(*base)
        for d in range(3):
            with_d = shifted(base, d)
            total = total + heat[d] * (double * squared(with_d) - 5.0 * product(*with_d))
        return total

    def with_heat(base, d):
        at = shifted(base, d)
        fourth = None
        for e in range(3):
            for f in range(3):
                term = product(*shifted(shifted(at, e, 2), f, 2))
                fourth = term if fourth is None else fourth + term
        return heat[d] * (double * fourth - 5.0 * squared(at))

    zero = (0, 0, 0)
    none = amount * whole(zero)
    one = [amount * whole(shifted(zero, d)) for d in range(3)]
    two = squared(zero)
    for d in range(3):
        two = two + with_heat(zero, d)
    two = amount * two
    square = flow[0] * flow[0] + flow[1] * flow[1] + flow[2] * flow[2]
    momentum = [one[d] + flow[d] * none for d in range(3)]
    trace = (
        two
        + 2.0 * (flow[0] * one[0] + flow[1] * one[1] + flow[2] * one[2])
        + square * none
    )
    return [none] + momentum + [trace]


def kernel(
    groups,
    digits,
    cells,
    state_ref,
    kind_ref,
    boundary_ref,
    table_ref,
    out_ref,
    macro_ref,
    raw,
    h_first,
    h_second,
    moved,
    halo,
    acc,
    edge,
    got_edge,
    part,
    got_a,
    mine,
    got_b,
    gathered,
    gauss,
    bend,
    tilt,
    keep_ref,
    input_sem,
    send_sem,
    recv_sem,
    edge_send,
    edge_recv,
    halo_send,
    halo_recv,
):
    points = RUN * digits
    vel = lax.axis_index("vel")
    cell = lax.axis_index("cell")
    jc = lax.rem(vel, digits)
    jb = lax.rem(vel // digits, digits)
    ja = vel // (digits * digits)
    lo = lax.rem(vel, 2)
    row = lax.rem(vel // 2, 8)
    col = vel // 16
    here = col * 2 + lo
    up = lax.rem(cell + 1, cells)
    down = lax.rem(cell + cells - 1, cells)

    def peer_a(other):
        return ((other // 2) * 16 + row * 2 + lax.rem(other, 2), cell)

    def peer_b(other):
        return (col * 16 + other * 2 + lo, cell)

    load = pltpu.make_async_copy(state_ref, raw, input_sem)
    load.start()
    barrier = pltpu.get_barrier_semaphore()
    for other in (up, down):
        pl.semaphore_signal(barrier, inc=1, device_id=(vel, other), device_id_type=MESH)
    if groups:
        for k in range(1, 8):
            pl.semaphore_signal(
                barrier, inc=1, device_id=peer_a(lax.rem(here + k, 8)), device_id_type=MESH
            )
            pl.semaphore_signal(
                barrier, inc=1, device_id=peer_b(lax.rem(row + k, 8)), device_id_type=MESH
            )
    pl.semaphore_wait(barrier, 16 if groups else 2)

    lane = lax.broadcasted_iota(jnp.int32, (8, 128), 1)
    sub = lax.broadcasted_iota(jnp.int32, (8, 128), 0)
    in_z = lax.rem(lane, 32)
    z_first, z_last = in_z == 0, in_z == 31
    y_low, y_high = lane < 32, lane >= 96
    y_first, y_last = sub == 0, sub == 7
    has_down = jnp.where(cell > 0, 1.0, 0.0).astype(jnp.float32)
    has_up = jnp.where(cell < cells - 1, 1.0, 0.0).astype(jnp.float32)

    def speed(m, digit):
        return table_ref[4 * m + digit] if digits == 4 else table_ref[m]

    def weight(m, digit):
        return table_ref[points + 4 * m + digit] if digits == 4 else table_ref[points + m]

    def courant(m, digit):
        return table_ref[2 * points + 4 * m + digit] if digits == 4 else table_ref[2 * points + m]

    def run_sums(values):
        sums = None
        for mc, value in enumerate(values):
            sz = speed(mc, jc)
            terms = [weight(mc, jc) * value]
            for _ in range(3):
                terms.append(sz * terms[-1])
            sums = terms if sums is None else [x + y for x, y in zip(sums, terms)]
        return sums

    def add_moments(ref, place, sums, ma, mb, factor):
        sx, sy = speed(ma, ja), speed(mb, jb)
        w = weight(ma, ja) * weight(mb, jb) * factor
        wx, wy = w * sx, w * sy
        t0, t1, t2, t3 = sums
        plane_square = sx * sx + sy * sy
        both = plane_square * t0 + t2
        rows = [
            w * t0,
            wx * t0,
            wy * t0,
            w * t1,
            (wx * sx) * t0,
            (wy * sy) * t0,
            w * t2,
            (wx * sy) * t0,
            wx * t1,
            wy * t1,
            wx * both,
            wy * both,
            w * (plane_square * t1 + t3),
        ]
        for r in range(13):
            ref[r, place] += rows[r]

    def shift_y(value, positive):
        turned = pltpu.roll(value, 32 if positive else 96, 1)
        carried = pltpu.roll(turned, 1 if positive else 7, 0)
        edge_rows, lanes = (y_first, y_low) if positive else (y_last, y_high)
        return jnp.where(lanes, jnp.where(edge_rows, 0.0, carried), turned)

    def shift_z(value, positive):
        turned = pltpu.roll(value, 1 if positive else 127, 1)
        return jnp.where(z_first if positive else z_last, 0.0, turned)

    def relaxed(i, ma, mb, plane, pi, outer):
        base = gauss[ma, plane] * gauss[RUN + mb, plane]
        bend_xy = bend[ma, plane] + bend[RUN + mb, plane]
        tilt_xy = tilt[ma, plane] + tilt[RUN + mb, plane]
        keep = keep_ref[plane]
        values = []
        if outer:
            kx = courant(ma, ja) * jnp.where(pi == 1, has_down, has_up)
        for mc in range(RUN):
            node = i * RUN + mc
            value = moved[plane, node]
            if outer:
                value = value + kx * halo[outer - 1, pi, node - pi * HALF]
            t = (tilt_xy + tilt[2 * RUN + mc, plane]) * (bend_xy + bend[2 * RUN + mc, plane])
            values.append(keep * value + (base * gauss[2 * RUN + mc, plane]) * (1.0 + t))
        return values

    def new_plane(step, i, ma, mb, plane, pi, outer):
        if step == 0:
            return [
                raw[pl.ds((i * RUN + mc) * 16 + plane, 8, stride=2), :] for mc in range(RUN)
            ]
        return relaxed(i, ma, mb, plane, pi, step if outer else 0)

    def send_edges(step, held):
        copies = []
        for pi, other in ((1, up), (0, down)):
            copies.append(
                pltpu.make_async_remote_copy(
                    src_ref=edge.at[step, pi],
                    dst_ref=got_edge.at[step, pi],
                    send_sem=edge_send.at[step, pi],
                    recv_sem=edge_recv.at[step, pi],
                    device_id=(vel, other),
                    device_id_type=MESH,
                )
            )
        for pi, other in ((1, up), (0, down)):
            copies.append(
                pltpu.make_async_remote_copy(
                    src_ref=held.at[pi, pl.ds(pi * HALF, HALF)],
                    dst_ref=halo.at[step, pi],
                    send_sem=halo_send.at[step, pi],
                    recv_sem=halo_recv.at[step, pi],
                    device_id=(vel, other),
                    device_id_type=MESH,
                )
            )
        for copy in copies:
            copy.start()
        return copies[:2], copies[2:]

    def exchange(step, phase, source, target, index, peer):
        copies = []
        for k in range(1, 8):
            other = lax.rem(index + k, 8)
            copy = pltpu.make_async_remote_copy(
                src_ref=source(other),
                dst_ref=target,
                send_sem=send_sem.at[step, phase, k - 1],
                recv_sem=recv_sem.at[step, phase, k - 1],
                device_id=peer(other),
                device_id_type=MESH,
            )
            copy.start()
            copies.append(copy)
        return copies

    def slice_rows(index):
        return pl.ds(pl.multiple_of(index * ROWS, ROWS), ROWS)

    def parameters_of(step, index, total_ref):
        moment = [total_ref[pl.ds(2 * r, 2), :] for r in range(13)]
        kind = kind_ref[pl.ds(2 * index, 2), :]
        boundary = [boundary_ref[r] for r in range(6)]
        rows = step_parameters(moment, kind, boundary)
        for r in range(ROWS // 2):
            value = rows[r] if r < len(rows) else jnp.zeros((2, 128), jnp.float32)
            gathered[step, pl.ds(index * ROWS + 2 * r, 2), :] = value

    def all_sums(step):
        for r in range(ROWS // 2):
            for p in range(2):
                value = acc[r, p] if r < 13 else jnp.zeros((8, 128), jnp.float32)
                if r < 13:
                    mask = has_down if p == 0 else has_up
                    value = value + mask * got_edge[step, 1 - p, r]
                part[step, pl.ds(2 * r + p, 8, stride=ROWS), :] = value
        if not groups:
            for index in range(8):
                mine[step] = part[step, pl.ds(index * ROWS, ROWS), :]
                parameters_of(step, index, mine.at[step])
            return
        copies = exchange(
            step, 0, lambda other: part.at[step, slice_rows(other)], got_a.at[step, here], here, peer_a
        )
        got_a[step, here] = part[step, slice_rows(here), :]
        for copy in copies:
            copy.wait()
        total = got_a[step, 0]
        for k in range(1, 8):
            total = total + got_a[step, k]
        mine[step] = total
        copies = exchange(
            step, 1, lambda other: mine.at[step], got_b.at[step, row], row, peer_b
        )
        got_b[step, row] = total
        for copy in copies:
            copy.wait()
        total = got_b[step, 0]
        for k in range(1, 8):
            total = total + got_b[step, k]
        acc_rows = got_b.at[step, row]
        acc_rows[...] = total
        parameters_of(step, here, acc_rows)
        block = gathered.at[step, slice_rows(here)]
        copies = exchange(step, 2, lambda other: block, block, here, peer_a)
        for copy in copies:
            copy.wait()

    def gathered_rows(step, r):
        return [gathered[step, pl.ds(2 * r + p, 8, stride=ROWS), :] for p in range(2)]

    def build_tables(step):
        keep, amount, *rest = [gathered_rows(step, r) for r in range(9)]
        for p in range(2):
            keep_ref[p] = keep[p]

        def fill(m, carry):
            for d, digit in enumerate((ja, jb, jc)):
                s = speed(m, digit)
                for p in range(2):
                    c = s - rest[d][p]
                    inverse = rest[3][p]
                    scaled = c * c * inverse
                    value = jnp.exp(-scaled)
                    lift = scaled + scaled
                    if d == 0:
                        value = value * amount[p]
                        lift = lift - 5.0
                    gauss[d * RUN + m, p] = value
                    bend[d * RUN + m, p] = lift
                    tilt[d * RUN + m, p] = c * rest[4 + d][p]
            return carry

        lax.fori_loop(0, RUN, fill, 0)

    load.wait()
    for step in range(STEPS):
        held = h_first if step == 0 else h_second
        edge[step] = jnp.zeros(edge.shape[1:], jnp.float32)
        acc[...] = jnp.zeros(acc.shape, jnp.float32)

        def inner(i, carry, step=step, held=held):
            ma, mb = i // RUN, lax.rem(i, RUN)
            pi = ma // (RUN // 2)
            values = new_plane(step, i, ma, mb, pi, pi, False)
            for mc in range(RUN):
                held[pi, i * RUN + mc] = values[mc]
            add_moments(edge.at[step, pi], slice(None), run_sums(values), ma, mb, courant(ma, ja))
            return carry

        lax.fori_loop(0, PAIRS, inner, 0)
        edges, halos = send_edges(step, held)
        if step > 0:
            for copy in halos_before:
                copy.wait()

        def outer(i, carry, step=step, held=held):
            ma, mb = i // RUN, lax.rem(i, RUN)
            pi = ma // (RUN // 2)
            values = new_plane(step, i, ma, mb, 1 - pi, pi, True)
            for mc in range(RUN):
                held[1 - pi, i * RUN + mc] = values[mc]
            return carry

        lax.fori_loop(0, PAIRS, outer, 0)

        for half in range(2):

            def transport(j, carry, half=half, held=held):
                ma = j // (RUN // 2)
                mb = half * (RUN // 2) + lax.rem(j, RUN // 2)
                pi = ma // (RUN // 2)
                i = ma * RUN + mb
                kx, ky = courant(ma, ja), courant(mb, jb)
                at_inner, at_outer = [], []
                for mc in range(RUN):
                    node = i * RUN + mc
                    kz = courant(mc, jc)
                    stay = 1.0 - (kx + ky + kz)
                    near, far = held[pi, node], held[1 - pi, node]

                    def flat(value):
                        return (
                            stay * value
                            + ky * shift_y(value, half == 1)
                            + kz * shift_z(value, mc >= RUN // 2)
                        )

                    at_inner.append(flat(near) + kx * far)
                    at_outer.append(flat(far))
                    moved[pi, node] = at_inner[-1]
                    moved[1 - pi, node] = at_outer[-1]
                add_moments(acc, pi, run_sums(at_inner), ma, mb, 1.0)
                add_moments(acc, 1 - pi, run_sums(at_outer), ma, mb, 1.0)
                return carry

            lax.fori_loop(0, PAIRS // 2, transport, 0)
        for copy in edges:
            copy.wait()
        all_sums(step)
        build_tables(step)
        halos_before = halos

    for copy in halos_before:
        copy.wait()

    def last(i, carry):
        ma, mb = i // RUN, lax.rem(i, RUN)
        pi = ma // (RUN // 2)
        for plane, is_outer in ((pi, 0), (1 - pi, STEPS)):
            values = relaxed(i, ma, mb, plane, pi, is_outer)
            for mc in range(RUN):
                out_ref[pl.ds((i * RUN + mc) * 16 + plane, 8, stride=2), :] = values[mc]
        return carry

    lax.fori_loop(0, PAIRS, last, 0)

    final = STEPS - 1
    for p in range(2):
        keep, amount, ux, uy, uz, inverse, qx, qy, qz, *old = [
            gathered_rows(final, r)[p] for r in range(14)
        ]
        flow, heat = (ux, uy, uz), (qx, qy, qz)

        def sums(a, carry):
            s, w = table_ref[a], table_ref[points + a]
            result = []
            for d in range(3):
                c = s - flow[d]
                term = w * jnp.exp(-(c * c * inverse))
                for n in range(6):
                    result.append(carry[d * 6 + n] + term)
                    term = term * c
            return tuple(result)

        power = lax.fori_loop(
            0, points, sums, tuple(jnp.zeros((8, 128), jnp.float32) for _ in range(18))
        )
        power = [power[d * 6 : d * 6 + 6] for d in range(3)]
        added = added_moments(power, amount, flow, inverse, heat)
        density, mx, my, mz, trace = [keep * x + y for x, y in zip(old, added)]
        u = [mx / density, my / density, mz / density]
        square = u[0] * u[0] + u[1] * u[1] + u[2] * u[2]
        result = [density] + u + [(trace / density - square) / 3.0]
        for r in range(5):
            macro_ref[pl.ds(r * 16 + p, 8, stride=2), :] = result[r]


def interleaved(array):
    lead = array.shape[:-2]
    return array.reshape(lead + (2, 8, 128)).swapaxes(-3, -2).reshape(-1, 128)


def restored(array, lead):
    return array.reshape((lead, 8, 2, 128)).swapaxes(1, 2).reshape(lead, 2, 1024)


def shards(groups, digits, cells, state_init, cell_kind, boundary_state):
    vmem = functools.partial(pl.BlockSpec, memory_space=pltpu.VMEM)
    smem = functools.partial(pl.BlockSpec, memory_space=pltpu.SMEM)
    table = jnp.asarray(one_dimensional_tables(RUN * digits), jnp.float32)
    f32 = jnp.float32
    state, macro = pl.pallas_call(
        functools.partial(kernel, groups, digits, cells),
        out_shape=(
            jax.ShapeDtypeStruct((NODES * 16, 128), f32),
            jax.ShapeDtypeStruct((80, 128), f32),
        ),
        in_specs=[pl.BlockSpec(memory_space=pl.ANY), vmem(), smem(), smem()],
        out_specs=(vmem(), vmem()),
        scratch_shapes=[
            pltpu.VMEM((NODES * 16, 128), f32),
            pltpu.VMEM((2, NODES, 8, 128), f32),
            pltpu.VMEM((2, NODES, 8, 128), f32),
            pltpu.VMEM((2, NODES, 8, 128), f32),
            pltpu.VMEM((STEPS, 2, HALF, 8, 128), f32),
            pltpu.VMEM((13, 2, 8, 128), f32),
            pltpu.VMEM((STEPS, 2, 13, 8, 128), f32),
            pltpu.VMEM((STEPS, 2, 13, 8, 128), f32),
            pltpu.VMEM((STEPS, 8 * ROWS, 128), f32),
            pltpu.VMEM((STEPS, 8, ROWS, 128), f32),
            pltpu.VMEM((STEPS, ROWS, 128), f32),
            pltpu.VMEM((STEPS, 8, ROWS, 128), f32),
            pltpu.VMEM((STEPS, 8 * ROWS, 128), f32),
            pltpu.VMEM((3 * RUN, 2, 8, 128), f32),
            pltpu.VMEM((3 * RUN, 2, 8, 128), f32),
            pltpu.VMEM((3 * RUN, 2, 8, 128), f32),
            pltpu.VMEM((2, 8, 128), f32),
            pltpu.SemaphoreType.DMA,
            pltpu.SemaphoreType.DMA((STEPS, 3, 7)),
            pltpu.SemaphoreType.DMA((STEPS, 3, 7)),
            pltpu.SemaphoreType.DMA((STEPS, 2)),
            pltpu.SemaphoreType.DMA((STEPS, 2)),
            pltpu.SemaphoreType.DMA((STEPS, 2)),
            pltpu.SemaphoreType.DMA((STEPS, 2)),
        ],
        compiler_params=pltpu.CompilerParams(
            collective_id=0, has_side_effects=True, vmem_limit_bytes=40 * 1024 * 1024
        ),
    )(interleaved(state_init), interleaved(cell_kind), boundary_state, table)
    return restored(state, NODES), restored(macro, 5)


def solution(mesh):
    in_specs = (P("vel", "cell", None), P("cell", None), P())
    out_specs = (P("vel", "cell", None), P(None, "cell", None))
    body = functools.partial(shards, True, 4, 8)
    return jax.shard_map(body, mesh=mesh, in_specs=in_specs, out_specs=out_specs, check_vma=False)
```

```python
import functools

import jax
import jax.numpy as jnp
import numpy as np
from jax import lax
from jax.experimental import pallas as pl
from jax.experimental.pallas import tpu as pltpu
from jax.sharding import PartitionSpec as P

QUAD_ABSCISSAE = 24
RUN = 6
STEPS = 2


MOMENTUM_RATIO = 2.0 / 3.0
SHEAR_EXPONENT = 0.81
SHEAR_REFERENCE = 0.05
TIME_INCREMENT = 0.03125

NODES = RUN * RUN * RUN
HALF = NODES // 2
PAIRS = RUN * RUN
USED = 26
ROWS = 32
MESH = pl.DeviceIdType.MESH


def hermite_rule(points):
    start_value = np.pi ** (-0.25)
    node_list = np.zeros(points)
    weight_list = np.zeros(points)
    guess_root = 0.0
    slope_value = 1.0
    for index in range((points + 1) // 2):
        if index == 0:
            guess_root = np.sqrt(2.0 * points + 1.0) - 1.85575 * (2.0 * points + 1.0) ** (-0.16667)
        elif index == 1:
            guess_root = guess_root - 1.14 * points**0.426 / guess_root
        elif index == 2:
            guess_root = 1.86 * guess_root - 0.86 * node_list[0]
        elif index == 3:
            guess_root = 1.91 * guess_root - 0.91 * node_list[1]
        else:
            guess_root = 2.0 * guess_root - node_list[index - 2]
        for sweep in range(60):
            poly_now = start_value
            poly_prev = 0.0
            for degree in range(points):
                poly_old = poly_prev
                poly_prev = poly_now
                poly_now = (
                    guess_root * np.sqrt(2.0 / (degree + 1)) * poly_prev
                    - np.sqrt(degree / (degree + 1.0)) * poly_old
                )
            slope_value = np.sqrt(2.0 * points) * poly_prev
            guess_root = guess_root - poly_now / slope_value
        node_list[index] = guess_root
        node_list[points - 1 - index] = -guess_root
        weight_list[index] = 2.0 / (slope_value * slope_value)
        weight_list[points - 1 - index] = weight_list[index]
    return (node_list[::-1].copy(), weight_list[::-1].copy())


def one_dimensional_tables(points):
    abscissa, weights = hermite_rule(points)
    speed = np.sqrt(2.0) * abscissa
    weight = weights * np.exp(abscissa * abscissa) / np.sqrt(np.pi)
    return np.concatenate([speed, weight, TIME_INCREMENT * np.abs(speed)])


def step_parameters(moment, kind, boundary):
    density = moment[0]
    first = moment[1:4]
    flow = [value / density for value in first]
    trace = moment[4] + moment[5] + moment[6]
    square = flow[0] * flow[0] + flow[1] * flow[1] + flow[2] * flow[2]
    temperature = (trace / density - square) / 3.0
    along = flow[0] * first[0] + flow[1] * first[1] + flow[2] * first[2]
    pairs = ((4, 7, 8), (7, 5, 9), (8, 9, 6))
    heat = []
    for d in range(3):
        tensor = (
            moment[pairs[d][0]] * flow[0]
            + moment[pairs[d][1]] * flow[1]
            + moment[pairs[d][2]] * flow[2]
        )
        heat.append(
            0.5
            * (
                moment[10 + d]
                - 2.0 * tensor
                + square * first[d]
                - flow[d] * trace
                + 2.0 * flow[d] * along
                - flow[d] * square * density
            )
        )
    pressure = density * temperature
    rate = (
        TIME_INCREMENT
        * pressure
        / (SHEAR_REFERENCE * jnp.exp(SHEAR_EXPONENT * jnp.log(temperature)))
    )
    keep = 1.0 / (1.0 + rate)
    scale = (1.0 - MOMENTUM_RATIO) / (5.0 * pressure * temperature)

    def pick(fluid, wall, inlet, outlet):
        return jnp.where(
            kind == 0, fluid, jnp.where(kind == 1, wall, jnp.where(kind == 2, inlet, outlet))
        )

    level = pick(temperature, boundary[5], boundary[4], 1.0)
    amount = pick(density * rate * keep, density, boundary[0], 0.0)
    return (
        [pick(keep, 0.0, 0.0, 1.0), amount / (level * jnp.sqrt(level))]
        + [pick(flow[d], 0.0, boundary[1 + d], 0.0) for d in range(3)]
        + [0.5 / level]
        + [pick(heat[d] * scale, 0.0, 0.0, 0.0) for d in range(3)]
        + [density, first[0], first[1], first[2], trace]
    )


def added_moments(power, amount, flow, inverse, heat):
    planes = {}

    def product(i, j, k):
        if (i, j) not in planes:
            planes[i, j] = power[0][i] * power[1][j]
        return planes[i, j] * power[2][k]

    def shifted(base, d, n=1):
        return tuple(base[e] + (n if e == d else 0) for e in range(3))

    def squared(base):
        return product(*shifted(base, 0, 2)) + product(*shifted(base, 1, 2)) + product(*shifted(base, 2, 2))

    double = inverse + inverse

    def whole(base):
        total = product(*base)
        for d in range(3):
            with_d = shifted(base, d)
            total = total + heat[d] * (double * squared(with_d) - 5.0 * product(*with_d))
        return total

    def with_heat(base, d):
        at = shifted(base, d)
        fourth = None
        for e in range(3):
            for f in range(3):
                term = product(*shifted(shifted(at, e, 2), f, 2))
                fourth = term if fourth is None else fourth + term
        return heat[d] * (double * fourth - 5.0 * squared(at))

    zero = (0, 0, 0)
    none = amount * whole(zero)
    one = [amount * whole(shifted(zero, d)) for d in range(3)]
    two = squared(zero)
    for d in range(3):
        two = two + with_heat(zero, d)
    two = amount * two
    square = flow[0] * flow[0] + flow[1] * flow[1] + flow[2] * flow[2]
    momentum = [one[d] + flow[d] * none for d in range(3)]
    trace = (
        two
        + 2.0 * (flow[0] * one[0] + flow[1] * one[1] + flow[2] * one[2])
        + square * none
    )
    return [none] + momentum + [trace]


def kernel(
    groups,
    digits,
    cells,
    state_ref,
    kind_hbm,
    boundary_ref,
    out_ref,
    macro_ref,
    kind_ref,
    table_ref,
    raw,
    h_first,
    h_second,
    moved,
    halo,
    acc,
    edge,
    got_edge,
    part,
    got_a,
    mine,
    got_b,
    gathered,
    gauss,
    bend,
    tilt,
    keep_ref,
    input_sem,
    send_sem,
    recv_sem,
    edge_send,
    edge_recv,
    halo_send,
    halo_recv,
):
    points = RUN * digits
    vel = lax.axis_index("vel")
    cell = lax.axis_index("cell")
    jc = lax.rem(vel, digits)
    jb = lax.rem(vel // digits, digits)
    ja = vel // (digits * digits)
    lo = lax.rem(vel, 2)
    row = lax.rem(vel // 2, 8)
    col = vel // 16
    here = col * 2 + lax.rem(row, 2)
    there = (row // 2) * 2 + lo
    up = lax.rem(cell + 1, cells)
    down = lax.rem(cell + cells - 1, cells)

    def peer_a(other):
        return ((other // 2) * 16 + (row // 2 * 2 + lax.rem(other, 2)) * 2 + lo, cell)

    def peer_b(other):
        return (col * 16 + (other // 2 * 2 + lax.rem(row, 2)) * 2 + lax.rem(other, 2), cell)

    loads = [
        pltpu.make_async_copy(state_ref, raw, input_sem.at[0]),
        pltpu.make_async_copy(kind_hbm, kind_ref, input_sem.at[1]),
    ]
    barrier = pltpu.get_barrier_semaphore()
    for other in (up, down):
        pl.semaphore_signal(barrier, inc=1, device_id=(vel, other), device_id_type=MESH)
    if groups:
        for k in range(1, 8):
            pl.semaphore_signal(
                barrier, inc=1, device_id=peer_a(lax.rem(here + k, 8)), device_id_type=MESH
            )
            pl.semaphore_signal(
                barrier, inc=1, device_id=peer_b(lax.rem(there + k, 8)), device_id_type=MESH
            )
    for copy in loads:
        copy.start()
    for index, value in enumerate(one_dimensional_tables(points)):
        table_ref[index] = jnp.float32(value)

    lane = lax.broadcasted_iota(jnp.int32, (8, 128), 1)
    sub = lax.broadcasted_iota(jnp.int32, (8, 128), 0)
    in_z = lax.rem(lane, 32)
    z_first, z_last = in_z == 0, in_z == 31
    y_low, y_high = lane < 32, lane >= 96
    y_first, y_last = sub == 0, sub == 7
    has_down = jnp.where(cell > 0, 1.0, 0.0).astype(jnp.float32)
    has_up = jnp.where(cell < cells - 1, 1.0, 0.0).astype(jnp.float32)

    def speed(m, digit):
        return table_ref[4 * m + digit] if digits == 4 else table_ref[m]

    def weight(m, digit):
        return table_ref[points + 4 * m + digit] if digits == 4 else table_ref[points + m]

    def courant(m, digit):
        return table_ref[2 * points + 4 * m + digit] if digits == 4 else table_ref[2 * points + m]

    def run_sums(values):
        sums = None
        for mc, value in enumerate(values):
            sz = speed(mc, jc)
            terms = [weight(mc, jc) * value]
            for _ in range(3):
                terms.append(sz * terms[-1])
            sums = terms if sums is None else [x + y for x, y in zip(sums, terms)]
        return sums

    def add_moments(ref, place, sums, ma, mb, factor):
        sx, sy = speed(ma, ja), speed(mb, jb)
        w = weight(ma, ja) * weight(mb, jb) * factor
        wx, wy = w * sx, w * sy
        t0, t1, t2, t3 = sums
        plane_square = sx * sx + sy * sy
        both = plane_square * t0 + t2
        rows = [
            w * t0,
            wx * t0,
            wy * t0,
            w * t1,
            (wx * sx) * t0,
            (wy * sy) * t0,
            w * t2,
            (wx * sy) * t0,
            wx * t1,
            wy * t1,
            wx * both,
            wy * both,
            w * (plane_square * t1 + t3),
        ]
        for r in range(13):
            ref[r, place] += rows[r]

    def shift_y(value, positive):
        turned = pltpu.roll(value, 32 if positive else 96, 1)
        carried = pltpu.roll(turned, 1 if positive else 7, 0)
        edge_rows, lanes = (y_first, y_low) if positive else (y_last, y_high)
        return jnp.where(lanes, jnp.where(edge_rows, 0.0, carried), turned)

    def shift_z(value, positive):
        turned = pltpu.roll(value, 1 if positive else 127, 1)
        return jnp.where(z_first if positive else z_last, 0.0, turned)

    def relaxed(i, ma, mb, plane, pi, outer):
        base = gauss[ma, plane] * gauss[RUN + mb, plane]
        bend_xy = bend[ma, plane] + bend[RUN + mb, plane]
        tilt_xy = tilt[ma, plane] + tilt[RUN + mb, plane]
        keep = keep_ref[plane]
        values = []
        if outer:
            kx = courant(ma, ja) * jnp.where(pi == 1, has_down, has_up)
        for mc in range(RUN):
            node = i * RUN + mc
            value = moved[plane, node]
            if outer:
                value = value + kx * halo[outer - 1, pi, node - pi * HALF]
            t = (tilt_xy + tilt[2 * RUN + mc, plane]) * (bend_xy + bend[2 * RUN + mc, plane])
            values.append(keep * value + (base * gauss[2 * RUN + mc, plane]) * (1.0 + t))
        return values

    def new_plane(step, i, ma, mb, plane, pi, outer):
        if step == 0:
            return [
                raw[pl.ds((i * RUN + mc) * 16 + plane, 8, stride=2), :] for mc in range(RUN)
            ]
        return relaxed(i, ma, mb, plane, pi, step if outer else 0)

    def send_edges(step, held):
        copies = []
        for pi, other in ((1, up), (0, down)):
            copies.append(
                pltpu.make_async_remote_copy(
                    src_ref=edge.at[step, pi],
                    dst_ref=got_edge.at[step, pi],
                    send_sem=edge_send.at[step, pi],
                    recv_sem=edge_recv.at[step, pi],
                    device_id=(vel, other),
                    device_id_type=MESH,
                )
            )
        for pi, other in ((1, up), (0, down)):
            copies.append(
                pltpu.make_async_remote_copy(
                    src_ref=held.at[pi, pl.ds(pi * HALF, HALF)],
                    dst_ref=halo.at[step, pi],
                    send_sem=halo_send.at[step, pi],
                    recv_sem=halo_recv.at[step, pi],
                    device_id=(vel, other),
                    device_id_type=MESH,
                )
            )
        for copy in copies:
            copy.start()
        return copies[:2], copies[2:]

    def exchange(step, phase, source, target, index, peer):
        copies = []
        for k in (4, 3, 5, 2, 6, 1, 7):
            other = lax.rem(index + k, 8)
            copy = pltpu.make_async_remote_copy(
                src_ref=source(other),
                dst_ref=target,
                send_sem=send_sem.at[step, phase, k - 1],
                recv_sem=recv_sem.at[step, phase, k - 1],
                device_id=peer(other),
                device_id_type=MESH,
            )
            copy.start()
            copies.append(copy)
        return copies

    def slice_rows(index, count):
        return pl.ds(pl.multiple_of(index * ROWS, ROWS), count)

    def parameters_of(step, index, total_ref):
        moment = [total_ref[pl.ds(2 * r, 2), :] for r in range(13)]
        kind = kind_ref[pl.ds(2 * index, 2), :]
        boundary = [boundary_ref[r] for r in range(6)]
        rows = step_parameters(moment, kind, boundary)
        for r in range(9 if step < STEPS - 1 else 14):
            gathered[step, pl.ds(index * ROWS + 2 * r, 2), :] = rows[r]

    def all_sums(step):
        for r in range(13):
            for p in range(2):
                mask = has_down if p == 0 else has_up
                value = acc[r, p] + mask * got_edge[step, 1 - p, r]
                part[step, pl.ds(2 * r + p, 8, stride=ROWS), :] = value
        if not groups:
            for index in range(8):
                mine[step] = part[step, pl.ds(index * ROWS, USED), :]
                parameters_of(step, index, mine.at[step])
            return
        copies = exchange(
            step, 0, lambda other: part.at[step, slice_rows(other, USED)], got_a.at[step, here], here, peer_a
        )
        got_a[step, here] = part[step, slice_rows(here, USED), :]
        for copy in copies:
            copy.wait()
        total = got_a[step, 0]
        for k in range(1, 8):
            total = total + got_a[step, k]
        mine[step] = total
        copies = exchange(
            step, 1, lambda other: mine.at[step], got_b.at[step, there], there, peer_b
        )
        got_b[step, there] = total
        for copy in copies:
            copy.wait()
        total = got_b[step, 0]
        for k in range(1, 8):
            total = total + got_b[step, k]
        acc_rows = got_b.at[step, there]
        acc_rows[...] = total
        parameters_of(step, here, acc_rows)
        block = gathered.at[step, slice_rows(here, 18 if step < STEPS - 1 else 28)]
        copies = exchange(step, 2, lambda other: block, block, here, peer_a)
        for copy in copies:
            copy.wait()

    def gathered_rows(step, r):
        return [gathered[step, pl.ds(2 * r + p, 8, stride=ROWS), :] for p in range(2)]

    def build_tables(step):
        keep, amount, *rest = [gathered_rows(step, r) for r in range(9)]
        for p in range(2):
            keep_ref[p] = keep[p]

        def fill(m, carry):
            for d, digit in enumerate((ja, jb, jc)):
                s = speed(m, digit)
                for p in range(2):
                    c = s - rest[d][p]
                    inverse = rest[3][p]
                    scaled = c * c * inverse
                    value = jnp.exp(-scaled)
                    lift = scaled + scaled
                    if d == 0:
                        value = value * amount[p]
                        lift = lift - 5.0
                    gauss[d * RUN + m, p] = value
                    bend[d * RUN + m, p] = lift
                    tilt[d * RUN + m, p] = c * rest[4 + d][p]
            return carry

        lax.fori_loop(0, RUN, fill, 0)

    for copy in loads:
        copy.wait()
    for step in range(STEPS):
        held = h_first if step == 0 else h_second
        edge[step] = jnp.zeros(edge.shape[1:], jnp.float32)
        acc[...] = jnp.zeros(acc.shape, jnp.float32)

        def inner(i, carry, step=step, held=held):
            ma, mb = i // RUN, lax.rem(i, RUN)
            pi = ma // (RUN // 2)
            values = new_plane(step, i, ma, mb, pi, pi, False)
            for mc in range(RUN):
                held[pi, i * RUN + mc] = values[mc]
            add_moments(edge.at[step, pi], slice(None), run_sums(values), ma, mb, courant(ma, ja))
            return carry

        lax.fori_loop(0, PAIRS, inner, 0, unroll=3)
        if step == 0:
            pl.semaphore_wait(barrier, 16 if groups else 2)
        edges, halos = send_edges(step, held)
        if step > 0:
            for copy in halos_before:
                copy.wait()

        def outer(i, carry, step=step, held=held):
            ma, mb = i // RUN, lax.rem(i, RUN)
            pi = ma // (RUN // 2)
            values = new_plane(step, i, ma, mb, 1 - pi, pi, True)
            for mc in range(RUN):
                held[1 - pi, i * RUN + mc] = values[mc]
            return carry

        lax.fori_loop(0, PAIRS, outer, 0, unroll=3)

        for half in range(2):

            def transport(j, carry, half=half, held=held):
                ma = j // (RUN // 2)
                mb = half * (RUN // 2) + lax.rem(j, RUN // 2)
                pi = ma // (RUN // 2)
                i = ma * RUN + mb
                kx, ky = courant(ma, ja), courant(mb, jb)
                at_inner, at_outer = [], []
                for mc in range(RUN):
                    node = i * RUN + mc
                    kz = courant(mc, jc)
                    stay = 1.0 - (kx + ky + kz)
                    near, far = held[pi, node], held[1 - pi, node]

                    def flat(value):
                        return (
                            stay * value
                            + ky * shift_y(value, half == 1)
                            + kz * shift_z(value, mc >= RUN // 2)
                        )

                    at_inner.append(flat(near) + kx * far)
                    at_outer.append(flat(far))
                    moved[pi, node] = at_inner[-1]
                    moved[1 - pi, node] = at_outer[-1]
                add_moments(acc, pi, run_sums(at_inner), ma, mb, 1.0)
                add_moments(acc, 1 - pi, run_sums(at_outer), ma, mb, 1.0)
                return carry

            lax.fori_loop(0, PAIRS // 2, transport, 0, unroll=3)
        for copy in edges:
            copy.wait()
        all_sums(step)
        build_tables(step)
        halos_before = halos

    for copy in halos_before:
        copy.wait()

    def last(i, carry):
        ma, mb = i // RUN, lax.rem(i, RUN)
        pi = ma // (RUN // 2)
        for plane, is_outer in ((pi, 0), (1 - pi, STEPS)):
            values = relaxed(i, ma, mb, plane, pi, is_outer)
            for mc in range(RUN):
                out_ref[pl.ds((i * RUN + mc) * 16 + plane, 8, stride=2), :] = values[mc]
        return carry

    lax.fori_loop(0, PAIRS, last, 0)

    final = STEPS - 1
    for p in range(2):
        keep, amount, ux, uy, uz, inverse, qx, qy, qz, *old = [
            gathered_rows(final, r)[p] for r in range(14)
        ]
        flow, heat = (ux, uy, uz), (qx, qy, qz)

        def sums(a, carry):
            s, w = table_ref[a], table_ref[points + a]
            result = []
            for d in range(3):
                c = s - flow[d]
                term = w * jnp.exp(-(c * c * inverse))
                for n in range(6):
                    result.append(carry[d * 6 + n] + term)
                    term = term * c
            return tuple(result)

        power = lax.fori_loop(
            0, points, sums, tuple(jnp.zeros((8, 128), jnp.float32) for _ in range(18))
        )
        power = [power[d * 6 : d * 6 + 6] for d in range(3)]
        added = added_moments(power, amount, flow, inverse, heat)
        density, mx, my, mz, trace = [keep * x + y for x, y in zip(old, added)]
        u = [mx / density, my / density, mz / density]
        square = u[0] * u[0] + u[1] * u[1] + u[2] * u[2]
        result = [density] + u + [(trace / density - square) / 3.0]
        for r in range(5):
            macro_ref[pl.ds(r * 16 + p, 8, stride=2), :] = result[r]


def interleaved(array):
    lead = array.shape[:-2]
    return array.reshape(lead + (2, 8, 128)).swapaxes(-3, -2).reshape(-1, 128)


def restored(array, lead):
    return array.reshape((lead, 8, 2, 128)).swapaxes(1, 2).reshape(lead, 2, 1024)


def shards(groups, digits, cells, state_init, cell_kind, boundary_state):
    vmem = functools.partial(pl.BlockSpec, memory_space=pltpu.VMEM)
    smem = functools.partial(pl.BlockSpec, memory_space=pltpu.SMEM)
    f32 = jnp.float32
    state, macro = pl.pallas_call(
        functools.partial(kernel, groups, digits, cells),
        out_shape=(
            jax.ShapeDtypeStruct((NODES * 16, 128), f32),
            jax.ShapeDtypeStruct((80, 128), f32),
        ),
        in_specs=[pl.BlockSpec(memory_space=pltpu.HBM), pl.BlockSpec(memory_space=pltpu.HBM), smem()],
        out_specs=(vmem(), vmem()),
        scratch_shapes=[
            pltpu.VMEM((16, 128), jnp.int32),
            pltpu.SMEM((3 * RUN * digits,), f32),
            pltpu.VMEM((NODES * 16, 128), f32),
            pltpu.VMEM((2, NODES, 8, 128), f32),
            pltpu.VMEM((2, NODES, 8, 128), f32),
            pltpu.VMEM((2, NODES, 8, 128), f32),
            pltpu.VMEM((STEPS, 2, HALF, 8, 128), f32),
            pltpu.VMEM((13, 2, 8, 128), f32),
            pltpu.VMEM((STEPS, 2, 13, 8, 128), f32),
            pltpu.VMEM((STEPS, 2, 13, 8, 128), f32),
            pltpu.VMEM((STEPS, 8 * ROWS, 128), f32),
            pltpu.VMEM((STEPS, 8, USED, 128), f32),
            pltpu.VMEM((STEPS, USED, 128), f32),
            pltpu.VMEM((STEPS, 8, USED, 128), f32),
            pltpu.VMEM((STEPS, 8 * ROWS, 128), f32),
            pltpu.VMEM((3 * RUN, 2, 8, 128), f32),
            pltpu.VMEM((3 * RUN, 2, 8, 128), f32),
            pltpu.VMEM((3 * RUN, 2, 8, 128), f32),
            pltpu.VMEM((2, 8, 128), f32),
            pltpu.SemaphoreType.DMA((2,)),
            pltpu.SemaphoreType.DMA((STEPS, 3, 7)),
            pltpu.SemaphoreType.DMA((STEPS, 3, 7)),
            pltpu.SemaphoreType.DMA((STEPS, 2)),
            pltpu.SemaphoreType.DMA((STEPS, 2)),
            pltpu.SemaphoreType.DMA((STEPS, 2)),
            pltpu.SemaphoreType.DMA((STEPS, 2)),
        ],
        compiler_params=pltpu.CompilerParams(
            collective_id=0, has_side_effects=True, vmem_limit_bytes=40 * 1024 * 1024
        ),
    )(interleaved(state_init), interleaved(cell_kind), boundary_state)
    return restored(state, NODES), restored(macro, 5)


def solution(mesh):
    in_specs = (P("vel", "cell", None), P("cell", None), P())
    out_specs = (P("vel", "cell", None), P(None, "cell", None))
    body = functools.partial(shards, True, 4, 8)
    return jax.shard_map(body, mesh=mesh, in_specs=in_specs, out_specs=out_specs, check_vma=False)
```

```python
import functools

import jax
import jax.numpy as jnp
import numpy as np
from jax import lax
from jax.experimental import pallas as pl
from jax.experimental.pallas import tpu as pltpu
from jax.sharding import PartitionSpec as P

QUAD_ABSCISSAE = 24
RUN = 6
STEPS = 2


MOMENTUM_RATIO = 2.0 / 3.0
SHEAR_EXPONENT = 0.81
SHEAR_REFERENCE = 0.05
TIME_INCREMENT = 0.03125

NODES = RUN * RUN * RUN
HALF = NODES // 2
PAIRS = RUN * RUN
USED = 26
ROWS = 32
ORDER = (4, 3, 5, 2, 6, 1, 7)
MESH = pl.DeviceIdType.MESH


def hermite_rule(points):
    start_value = np.pi ** (-0.25)
    node_list = np.zeros(points)
    weight_list = np.zeros(points)
    guess_root = 0.0
    slope_value = 1.0
    for index in range((points + 1) // 2):
        if index == 0:
            guess_root = np.sqrt(2.0 * points + 1.0) - 1.85575 * (2.0 * points + 1.0) ** (-0.16667)
        elif index == 1:
            guess_root = guess_root - 1.14 * points**0.426 / guess_root
        elif index == 2:
            guess_root = 1.86 * guess_root - 0.86 * node_list[0]
        elif index == 3:
            guess_root = 1.91 * guess_root - 0.91 * node_list[1]
        else:
            guess_root = 2.0 * guess_root - node_list[index - 2]
        for sweep in range(60):
            poly_now = start_value
            poly_prev = 0.0
            for degree in range(points):
                poly_old = poly_prev
                poly_prev = poly_now
                poly_now = (
                    guess_root * np.sqrt(2.0 / (degree + 1)) * poly_prev
                    - np.sqrt(degree / (degree + 1.0)) * poly_old
                )
            slope_value = np.sqrt(2.0 * points) * poly_prev
            guess_root = guess_root - poly_now / slope_value
        node_list[index] = guess_root
        node_list[points - 1 - index] = -guess_root
        weight_list[index] = 2.0 / (slope_value * slope_value)
        weight_list[points - 1 - index] = weight_list[index]
    return (node_list[::-1].copy(), weight_list[::-1].copy())


def one_dimensional_tables(points):
    abscissa, weights = hermite_rule(points)
    speed = np.sqrt(2.0) * abscissa
    weight = weights * np.exp(abscissa * abscissa) / np.sqrt(np.pi)
    return np.concatenate([speed, weight, TIME_INCREMENT * np.abs(speed)])


def step_parameters(moment, kind, boundary):
    density = moment[0]
    first = moment[1:4]
    flow = [value / density for value in first]
    trace = moment[4] + moment[5] + moment[6]
    square = flow[0] * flow[0] + flow[1] * flow[1] + flow[2] * flow[2]
    temperature = (trace / density - square) / 3.0
    along = flow[0] * first[0] + flow[1] * first[1] + flow[2] * first[2]
    pairs = ((4, 7, 8), (7, 5, 9), (8, 9, 6))
    heat = []
    for d in range(3):
        tensor = (
            moment[pairs[d][0]] * flow[0]
            + moment[pairs[d][1]] * flow[1]
            + moment[pairs[d][2]] * flow[2]
        )
        heat.append(
            0.5
            * (
                moment[10 + d]
                - 2.0 * tensor
                + square * first[d]
                - flow[d] * trace
                + 2.0 * flow[d] * along
                - flow[d] * square * density
            )
        )
    pressure = density * temperature
    rate = (
        TIME_INCREMENT
        * pressure
        / (SHEAR_REFERENCE * jnp.exp(SHEAR_EXPONENT * jnp.log(temperature)))
    )
    keep = 1.0 / (1.0 + rate)
    scale = (1.0 - MOMENTUM_RATIO) / (5.0 * pressure * temperature)

    def pick(fluid, wall, inlet, outlet):
        return jnp.where(
            kind == 0, fluid, jnp.where(kind == 1, wall, jnp.where(kind == 2, inlet, outlet))
        )

    level = pick(temperature, boundary[5], boundary[4], 1.0)
    amount = pick(density * rate * keep, density, boundary[0], 0.0)
    return (
        [pick(keep, 0.0, 0.0, 1.0), amount / (level * jnp.sqrt(level))]
        + [pick(flow[d], 0.0, boundary[1 + d], 0.0) for d in range(3)]
        + [0.5 / level]
        + [pick(heat[d] * scale, 0.0, 0.0, 0.0) for d in range(3)]
        + [density, first[0], first[1], first[2], trace]
    )


def added_moments(power, amount, flow, inverse, heat):
    planes = {}

    def product(i, j, k):
        if (i, j) not in planes:
            planes[i, j] = power[0][i] * power[1][j]
        return planes[i, j] * power[2][k]

    def shifted(base, d, n=1):
        return tuple(base[e] + (n if e == d else 0) for e in range(3))

    def squared(base):
        return product(*shifted(base, 0, 2)) + product(*shifted(base, 1, 2)) + product(*shifted(base, 2, 2))

    double = inverse + inverse

    def whole(base):
        total = product(*base)
        for d in range(3):
            with_d = shifted(base, d)
            total = total + heat[d] * (double * squared(with_d) - 5.0 * product(*with_d))
        return total

    def with_heat(base, d):
        at = shifted(base, d)
        fourth = None
        for e in range(3):
            for f in range(3):
                term = product(*shifted(shifted(at, e, 2), f, 2))
                fourth = term if fourth is None else fourth + term
        return heat[d] * (double * fourth - 5.0 * squared(at))

    zero = (0, 0, 0)
    none = amount * whole(zero)
    one = [amount * whole(shifted(zero, d)) for d in range(3)]
    two = squared(zero)
    for d in range(3):
        two = two + with_heat(zero, d)
    two = amount * two
    square = flow[0] * flow[0] + flow[1] * flow[1] + flow[2] * flow[2]
    momentum = [one[d] + flow[d] * none for d in range(3)]
    trace = (
        two
        + 2.0 * (flow[0] * one[0] + flow[1] * one[1] + flow[2] * one[2])
        + square * none
    )
    return [none] + momentum + [trace]


def kernel(
    digits,
    cells,
    state_ref,
    kind_hbm,
    boundary_ref,
    out_ref,
    macro_ref,
    kind_ref,
    table_ref,
    raw,
    h_first,
    h_second,
    moved,
    halo,
    acc,
    edge,
    edge_part,
    got_edge,
    edge_sum,
    part,
    got_a,
    mine,
    got_b,
    gathered,
    gauss,
    bend,
    tilt,
    keep_ref,
    input_sem,
    send_sem,
    recv_sem,
    edge_send,
    edge_recv,
    halo_send,
    halo_recv,
):
    points = RUN * digits
    vel = lax.axis_index("vel")
    cell = lax.axis_index("cell")
    jc = lax.rem(vel, digits)
    jb = lax.rem(vel // digits, digits)
    ja = vel // (digits * digits)
    lo = lax.rem(vel, 2)
    row = lax.rem(vel // 2, 8)
    col = vel // 16
    here = col * 2 + lax.rem(row, 2)
    there = (row // 2) * 2 + lo
    up = lax.rem(cell + 1, cells)
    down = lax.rem(cell + cells - 1, cells)

    def peer_a(other, slab):
        return ((other // 2) * 16 + (row // 2 * 2 + lax.rem(other, 2)) * 2 + lo, slab)

    def peer_b(other, slab):
        return (col * 16 + (other // 2 * 2 + lax.rem(row, 2)) * 2 + lax.rem(other, 2), slab)

    loads = [
        pltpu.make_async_copy(state_ref, raw, input_sem.at[0]),
        pltpu.make_async_copy(kind_hbm, kind_ref, input_sem.at[1]),
    ]
    barrier = pltpu.get_barrier_semaphore()
    greeted = [peer_a(lax.rem(here + k, 8), other) for k in range(8) for other in (up, down)]
    greeted += [peer_a(lax.rem(here + k, 8), cell) for k in range(1, 8)]
    greeted += [peer_b(lax.rem(there + k, 8), cell) for k in range(1, 8)]
    for device in greeted:
        pl.semaphore_signal(barrier, inc=1, device_id=device, device_id_type=MESH)
    for copy in loads:
        copy.start()
    for index, value in enumerate(one_dimensional_tables(points)):
        table_ref[index] = jnp.float32(value)

    lane = lax.broadcasted_iota(jnp.int32, (8, 128), 1)
    sub = lax.broadcasted_iota(jnp.int32, (8, 128), 0)
    in_z = lax.rem(lane, 32)
    z_first, z_last = in_z == 0, in_z == 31
    y_low, y_high = lane < 32, lane >= 96
    y_first, y_last = sub == 0, sub == 7
    has_down = jnp.where(cell > 0, 1.0, 0.0).astype(jnp.float32)
    has_up = jnp.where(cell < cells - 1, 1.0, 0.0).astype(jnp.float32)

    def speed(m, digit):
        return table_ref[4 * m + digit] if digits == 4 else table_ref[m]

    def weight(m, digit):
        return table_ref[points + 4 * m + digit] if digits == 4 else table_ref[points + m]

    def courant(m, digit):
        return table_ref[2 * points + 4 * m + digit] if digits == 4 else table_ref[2 * points + m]

    def run_sums(values):
        sums = None
        for mc, value in enumerate(values):
            sz = speed(mc, jc)
            terms = [weight(mc, jc) * value]
            for _ in range(3):
                terms.append(sz * terms[-1])
            sums = terms if sums is None else [x + y for x, y in zip(sums, terms)]
        return sums

    def add_moments(ref, place, sums, ma, mb, factor):
        sx, sy = speed(ma, ja), speed(mb, jb)
        w = weight(ma, ja) * weight(mb, jb) * factor
        wx, wy = w * sx, w * sy
        t0, t1, t2, t3 = sums
        plane_square = sx * sx + sy * sy
        both = plane_square * t0 + t2
        rows = [
            w * t0,
            wx * t0,
            wy * t0,
            w * t1,
            (wx * sx) * t0,
            (wy * sy) * t0,
            w * t2,
            (wx * sy) * t0,
            wx * t1,
            wy * t1,
            wx * both,
            wy * both,
            w * (plane_square * t1 + t3),
        ]
        for r in range(13):
            ref[r, place] += rows[r]

    def shift_y(value, positive):
        turned = pltpu.roll(value, 32 if positive else 96, 1)
        carried = pltpu.roll(turned, 1 if positive else 7, 0)
        edge_rows, lanes = (y_first, y_low) if positive else (y_last, y_high)
        return jnp.where(lanes, jnp.where(edge_rows, 0.0, carried), turned)

    def shift_z(value, positive):
        turned = pltpu.roll(value, 1 if positive else 127, 1)
        return jnp.where(z_first if positive else z_last, 0.0, turned)

    def relaxed(i, ma, mb, plane, pi, outer):
        base = gauss[ma, plane] * gauss[RUN + mb, plane]
        bend_xy = bend[ma, plane] + bend[RUN + mb, plane]
        tilt_xy = tilt[ma, plane] + tilt[RUN + mb, plane]
        keep = keep_ref[plane]
        values = []
        if outer:
            kx = courant(ma, ja) * jnp.where(pi == 1, has_down, has_up)
        for mc in range(RUN):
            node = i * RUN + mc
            value = moved[plane, node]
            if outer:
                value = value + kx * halo[outer - 1, pi, node - pi * HALF]
            t = (tilt_xy + tilt[2 * RUN + mc, plane]) * (bend_xy + bend[2 * RUN + mc, plane])
            values.append(keep * value + (base * gauss[2 * RUN + mc, plane]) * (1.0 + t))
        return values

    def new_plane(step, i, ma, mb, plane, pi, outer):
        if step == 0:
            return [
                raw[pl.ds((i * RUN + mc) * 16 + plane, 8, stride=2), :] for mc in range(RUN)
            ]
        return relaxed(i, ma, mb, plane, pi, step if outer else 0)

    def send_edges(step, held):
        copies = []
        for r in range(13):
            for pi in range(2):
                edge_part[step, pi, pl.ds(r, 8, stride=16), :] = edge[pi, r]
        for k in ORDER + (0,):
            other = lax.rem(here + k, 8)
            for pi, slab in ((1, up), (0, down)):
                copies.append(
                    pltpu.make_async_remote_copy(
                        src_ref=edge_part.at[step, pi, pl.ds(pl.multiple_of(other * 16, 16), 13)],
                        dst_ref=got_edge.at[step, pi, here],
                        send_sem=edge_send.at[step, pi, k],
                        recv_sem=edge_recv.at[step, pi, k],
                        device_id=peer_a(other, slab),
                        device_id_type=MESH,
                    )
                )
        for pi, other in ((1, up), (0, down)):
            copies.append(
                pltpu.make_async_remote_copy(
                    src_ref=held.at[pl.ds(pi * HALF, HALF)],
                    dst_ref=halo.at[step, pi],
                    send_sem=halo_send.at[step, pi],
                    recv_sem=halo_recv.at[step, pi],
                    device_id=(vel, other),
                    device_id_type=MESH,
                )
            )
        for copy in copies:
            copy.start()
        return copies[:16], copies[16:]

    def exchange(step, phase, source, target, index, peer):
        copies = []
        for k in ORDER:
            other = lax.rem(index + k, 8)
            copy = pltpu.make_async_remote_copy(
                src_ref=source(other),
                dst_ref=target,
                send_sem=send_sem.at[step, phase, k - 1],
                recv_sem=recv_sem.at[step, phase, k - 1],
                device_id=peer(other, cell),
                device_id_type=MESH,
            )
            copy.start()
            copies.append(copy)
        return copies

    def slice_rows(index, count):
        return pl.ds(pl.multiple_of(index * ROWS, ROWS), count)

    def parameters_of(step, index, total_ref):
        moment = [total_ref[pl.ds(r, 2, stride=13), :] for r in range(13)]
        kind = kind_ref[pl.ds(2 * index, 2), :]
        boundary = [boundary_ref[r] for r in range(6)]
        rows = step_parameters(moment, kind, boundary)
        for r in range(9 if step < STEPS - 1 else 14):
            gathered[step, pl.ds(index * ROWS + 2 * r, 2), :] = rows[r]

    def all_sums(step, edges):
        for r in range(13):
            for p in range(2):
                part[step, pl.ds(13 * p + r, 8, stride=ROWS), :] = acc[r, p]
        copies = exchange(
            step, 0, lambda other: part.at[step, slice_rows(other, USED)], got_a.at[step, here], here, peer_a
        )
        got_a[step, here] = part[step, slice_rows(here, USED), :]
        for copy in edges:
            copy.wait()
        for p in range(2):
            from_edge = got_edge[step, 1 - p, 0]
            for k in range(1, 8):
                from_edge = from_edge + got_edge[step, 1 - p, k]
            edge_sum[pl.ds(13 * p, 13), :] = from_edge * (has_down if p == 0 else has_up)
        for copy in copies:
            copy.wait()
        total = edge_sum[...]
        for k in range(8):
            total = total + got_a[step, k]
        mine[step] = total
        copies = exchange(
            step, 1, lambda other: mine.at[step], got_b.at[step, there], there, peer_b
        )
        got_b[step, there] = total
        for copy in copies:
            copy.wait()
        total = got_b[step, 0]
        for k in range(1, 8):
            total = total + got_b[step, k]
        acc_rows = got_b.at[step, there]
        acc_rows[...] = total
        parameters_of(step, here, acc_rows)
        block = gathered.at[step, slice_rows(here, 18 if step < STEPS - 1 else 28)]
        copies = exchange(step, 2, lambda other: block, block, here, peer_a)
        for copy in copies:
            copy.wait()

    def gathered_rows(step, r):
        return [gathered[step, pl.ds(2 * r + p, 8, stride=ROWS), :] for p in range(2)]

    def build_tables(step):
        keep, amount, *rest = [gathered_rows(step, r) for r in range(9)]
        for p in range(2):
            keep_ref[p] = keep[p]

        def fill(m, carry):
            for d, digit in enumerate((ja, jb, jc)):
                s = speed(m, digit)
                for p in range(2):
                    c = s - rest[d][p]
                    inverse = rest[3][p]
                    scaled = c * c * inverse
                    value = jnp.exp(-scaled)
                    lift = scaled + scaled
                    if d == 0:
                        value = value * amount[p]
                        lift = lift - 5.0
                    gauss[d * RUN + m, p] = value
                    bend[d * RUN + m, p] = lift
                    tilt[d * RUN + m, p] = c * rest[4 + d][p]
            return carry

        lax.fori_loop(0, RUN, fill, 0)

    for copy in loads:
        copy.wait()
    for step in range(STEPS):
        held = h_first if step == 0 else h_second
        edge[...] = jnp.zeros(edge.shape, jnp.float32)
        acc[...] = jnp.zeros(acc.shape, jnp.float32)

        def inner(i, carry, step=step, held=held):
            ma, mb = i // RUN, lax.rem(i, RUN)
            pi = ma // (RUN // 2)
            values = new_plane(step, i, ma, mb, pi, pi, False)
            for mc in range(RUN):
                held[i * RUN + mc] = values[mc]
            add_moments(edge.at[pi], slice(None), run_sums(values), ma, mb, courant(ma, ja))
            return carry

        lax.fori_loop(0, PAIRS, inner, 0, unroll=3)
        if step == 0:
            pl.semaphore_wait(barrier, len(greeted))
        edges, halos = send_edges(step, held)
        if step > 0:
            for copy in halos_before:
                copy.wait()

        for half in range(2):

            def transport(j, carry, half=half, step=step, held=held):
                ma = j // (RUN // 2)
                mb = half * (RUN // 2) + lax.rem(j, RUN // 2)
                pi = ma // (RUN // 2)
                i = ma * RUN + mb
                kx, ky = courant(ma, ja), courant(mb, jb)
                at_inner, at_outer = [], []
                values = new_plane(step, i, ma, mb, 1 - pi, pi, True)
                for mc in range(RUN):
                    node = i * RUN + mc
                    kz = courant(mc, jc)
                    stay = 1.0 - (kx + ky + kz)
                    near, far = held[node], values[mc]

                    def flat(value):
                        return (
                            stay * value
                            + ky * shift_y(value, half == 1)
                            + kz * shift_z(value, mc >= RUN // 2)
                        )

                    at_inner.append(flat(near) + kx * far)
                    at_outer.append(flat(far))
                    moved[pi, node] = at_inner[-1]
                    moved[1 - pi, node] = at_outer[-1]
                add_moments(acc, pi, run_sums(at_inner), ma, mb, 1.0)
                add_moments(acc, 1 - pi, run_sums(at_outer), ma, mb, 1.0)
                return carry

            lax.fori_loop(0, PAIRS // 2, transport, 0, unroll=6)
        all_sums(step, edges)
        build_tables(step)
        halos_before = halos

    for copy in halos_before:
        copy.wait()

    def last(i, carry):
        ma, mb = i // RUN, lax.rem(i, RUN)
        pi = ma // (RUN // 2)
        for plane, is_outer in ((pi, 0), (1 - pi, STEPS)):
            values = relaxed(i, ma, mb, plane, pi, is_outer)
            for mc in range(RUN):
                out_ref[pl.ds((i * RUN + mc) * 16 + plane, 8, stride=2), :] = values[mc]
        return carry

    lax.fori_loop(0, PAIRS, last, 0, unroll=3)

    final = STEPS - 1
    for p in range(2):
        keep, amount, ux, uy, uz, inverse, qx, qy, qz, *old = [
            gathered_rows(final, r)[p] for r in range(14)
        ]
        flow, heat = (ux, uy, uz), (qx, qy, qz)

        def sums(a, carry):
            s, w = table_ref[a], table_ref[points + a]
            result = []
            for d in range(3):
                c = s - flow[d]
                term = w * jnp.exp(-(c * c * inverse))
                for n in range(6):
                    result.append(carry[d * 6 + n] + term)
                    term = term * c
            return tuple(result)

        power = lax.fori_loop(
            0, points, sums, tuple(jnp.zeros((8, 128), jnp.float32) for _ in range(18)), unroll=4
        )
        power = [power[d * 6 : d * 6 + 6] for d in range(3)]
        added = added_moments(power, amount, flow, inverse, heat)
        density, mx, my, mz, trace = [keep * x + y for x, y in zip(old, added)]
        u = [mx / density, my / density, mz / density]
        square = u[0] * u[0] + u[1] * u[1] + u[2] * u[2]
        result = [density] + u + [(trace / density - square) / 3.0]
        for r in range(5):
            macro_ref[pl.ds(r * 16 + p, 8, stride=2), :] = result[r]


def interleaved(array):
    lead = array.shape[:-2]
    return array.reshape(lead + (2, 8, 128)).swapaxes(-3, -2).reshape(-1, 128)


def restored(array, lead):
    return array.reshape((lead, 8, 2, 128)).swapaxes(1, 2).reshape(lead, 2, 1024)


def shards(digits, cells, state_init, cell_kind, boundary_state):
    vmem = functools.partial(pl.BlockSpec, memory_space=pltpu.VMEM)
    smem = functools.partial(pl.BlockSpec, memory_space=pltpu.SMEM)
    f32 = jnp.float32
    state, macro = pl.pallas_call(
        functools.partial(kernel, digits, cells),
        out_shape=(
            jax.ShapeDtypeStruct((NODES * 16, 128), f32),
            jax.ShapeDtypeStruct((80, 128), f32),
        ),
        in_specs=[pl.BlockSpec(memory_space=pltpu.HBM), pl.BlockSpec(memory_space=pltpu.HBM), smem()],
        out_specs=(vmem(), vmem()),
        scratch_shapes=[
            pltpu.VMEM((16, 128), jnp.int32),
            pltpu.SMEM((3 * RUN * digits,), f32),
            pltpu.VMEM((NODES * 16, 128), f32),
            pltpu.VMEM((NODES, 8, 128), f32),
            pltpu.VMEM((NODES, 8, 128), f32),
            pltpu.VMEM((2, NODES, 8, 128), f32),
            pltpu.VMEM((STEPS, 2, HALF, 8, 128), f32),
            pltpu.VMEM((13, 2, 8, 128), f32),
            pltpu.VMEM((2, 13, 8, 128), f32),
            pltpu.VMEM((STEPS, 2, 8 * 16, 128), f32),
            pltpu.VMEM((STEPS, 2, 8, 13, 128), f32),
            pltpu.VMEM((USED, 128), f32),
            pltpu.VMEM((STEPS, 8 * ROWS, 128), f32),
            pltpu.VMEM((STEPS, 8, USED, 128), f32),
            pltpu.VMEM((STEPS, USED, 128), f32),
            pltpu.VMEM((STEPS, 8, USED, 128), f32),
            pltpu.VMEM((STEPS, 8 * ROWS, 128), f32),
            pltpu.VMEM((3 * RUN, 2, 8, 128), f32),
            pltpu.VMEM((3 * RUN, 2, 8, 128), f32),
            pltpu.VMEM((3 * RUN, 2, 8, 128), f32),
            pltpu.VMEM((2, 8, 128), f32),
            pltpu.SemaphoreType.DMA((2,)),
            pltpu.SemaphoreType.DMA((STEPS, 3, 7)),
            pltpu.SemaphoreType.DMA((STEPS, 3, 7)),
            pltpu.SemaphoreType.DMA((STEPS, 2, 8)),
            pltpu.SemaphoreType.DMA((STEPS, 2, 8)),
            pltpu.SemaphoreType.DMA((STEPS, 2)),
            pltpu.SemaphoreType.DMA((STEPS, 2)),
        ],
        compiler_params=pltpu.CompilerParams(
            collective_id=0, has_side_effects=True, vmem_limit_bytes=52 * 1024 * 1024
        ),
    )(interleaved(state_init), interleaved(cell_kind), boundary_state)
    return restored(state, NODES), restored(macro, 5)


def solution(mesh):
    in_specs = (P("vel", "cell", None), P("cell", None), P())
    out_specs = (P("vel", "cell", None), P(None, "cell", None))
    body = functools.partial(shards, 4, 8)
    return jax.shard_map(body, mesh=mesh, in_specs=in_specs, out_specs=out_specs, check_vma=False)
```

```python
import functools

import jax
import jax.numpy as jnp
import numpy as np
from jax import lax
from jax.experimental import pallas as pl
from jax.experimental.pallas import tpu as pltpu
from jax.sharding import PartitionSpec as P

QUAD_ABSCISSAE = 24
RUN = 6
STEPS = 2


MOMENTUM_RATIO = 2.0 / 3.0
SHEAR_EXPONENT = 0.81
SHEAR_REFERENCE = 0.05
TIME_INCREMENT = 0.03125

NODES = RUN * RUN * RUN
HALF = NODES // 2
EARLY = 88
PAIRS = RUN * RUN
USED = 26
ROWS = 32
ORDER = (4, 3, 5, 2, 6, 1, 7)
MESH = pl.DeviceIdType.MESH


def hermite_rule(points):
    start_value = np.pi ** (-0.25)
    node_list = np.zeros(points)
    weight_list = np.zeros(points)
    guess_root = 0.0
    slope_value = 1.0
    for index in range((points + 1) // 2):
        if index == 0:
            guess_root = np.sqrt(2.0 * points + 1.0) - 1.85575 * (2.0 * points + 1.0) ** (-0.16667)
        elif index == 1:
            guess_root = guess_root - 1.14 * points**0.426 / guess_root
        elif index == 2:
            guess_root = 1.86 * guess_root - 0.86 * node_list[0]
        elif index == 3:
            guess_root = 1.91 * guess_root - 0.91 * node_list[1]
        else:
            guess_root = 2.0 * guess_root - node_list[index - 2]
        for sweep in range(60):
            poly_now = start_value
            poly_prev = 0.0
            for degree in range(points):
                poly_old = poly_prev
                poly_prev = poly_now
                poly_now = (
                    guess_root * np.sqrt(2.0 / (degree + 1)) * poly_prev
                    - np.sqrt(degree / (degree + 1.0)) * poly_old
                )
            slope_value = np.sqrt(2.0 * points) * poly_prev
            guess_root = guess_root - poly_now / slope_value
        node_list[index] = guess_root
        node_list[points - 1 - index] = -guess_root
        weight_list[index] = 2.0 / (slope_value * slope_value)
        weight_list[points - 1 - index] = weight_list[index]
    return (node_list[::-1].copy(), weight_list[::-1].copy())


def one_dimensional_tables(points):
    abscissa, weights = hermite_rule(points)
    speed = np.sqrt(2.0) * abscissa
    weight = weights * np.exp(abscissa * abscissa) / np.sqrt(np.pi)
    return np.concatenate([speed, weight, TIME_INCREMENT * np.abs(speed)])


def step_parameters(moment, kind, boundary):
    density = moment[0]
    first = moment[1:4]
    flow = [value / density for value in first]
    trace = moment[4] + moment[5] + moment[6]
    square = flow[0] * flow[0] + flow[1] * flow[1] + flow[2] * flow[2]
    temperature = (trace / density - square) / 3.0
    along = flow[0] * first[0] + flow[1] * first[1] + flow[2] * first[2]
    pairs = ((4, 7, 8), (7, 5, 9), (8, 9, 6))
    heat = []
    for d in range(3):
        tensor = (
            moment[pairs[d][0]] * flow[0]
            + moment[pairs[d][1]] * flow[1]
            + moment[pairs[d][2]] * flow[2]
        )
        heat.append(
            0.5
            * (
                moment[10 + d]
                - 2.0 * tensor
                + square * first[d]
                - flow[d] * trace
                + 2.0 * flow[d] * along
                - flow[d] * square * density
            )
        )
    pressure = density * temperature
    rate = (
        TIME_INCREMENT
        * pressure
        / (SHEAR_REFERENCE * jnp.exp(SHEAR_EXPONENT * jnp.log(temperature)))
    )
    keep = 1.0 / (1.0 + rate)
    scale = (1.0 - MOMENTUM_RATIO) / (5.0 * pressure * temperature)

    def pick(fluid, wall, inlet, outlet):
        return jnp.where(
            kind == 0, fluid, jnp.where(kind == 1, wall, jnp.where(kind == 2, inlet, outlet))
        )

    level = pick(temperature, boundary[5], boundary[4], 1.0)
    amount = pick(density * rate * keep, density, boundary[0], 0.0)
    return (
        [pick(keep, 0.0, 0.0, 1.0), amount / (level * jnp.sqrt(level))]
        + [pick(flow[d], 0.0, boundary[1 + d], 0.0) for d in range(3)]
        + [0.5 / level]
        + [pick(heat[d] * scale, 0.0, 0.0, 0.0) for d in range(3)]
        + [density, first[0], first[1], first[2], trace]
    )


def added_moments(power, amount, flow, inverse, heat):
    planes = {}

    def product(i, j, k):
        if (i, j) not in planes:
            planes[i, j] = power[0][i] * power[1][j]
        return planes[i, j] * power[2][k]

    def shifted(base, d, n=1):
        return tuple(base[e] + (n if e == d else 0) for e in range(3))

    def squared(base):
        return product(*shifted(base, 0, 2)) + product(*shifted(base, 1, 2)) + product(*shifted(base, 2, 2))

    double = inverse + inverse

    def whole(base):
        total = product(*base)
        for d in range(3):
            with_d = shifted(base, d)
            total = total + heat[d] * (double * squared(with_d) - 5.0 * product(*with_d))
        return total

    def with_heat(base, d):
        at = shifted(base, d)
        fourth = None
        for e in range(3):
            for f in range(3):
                term = product(*shifted(shifted(at, e, 2), f, 2))
                fourth = term if fourth is None else fourth + term
        return heat[d] * (double * fourth - 5.0 * squared(at))

    zero = (0, 0, 0)
    none = amount * whole(zero)
    one = [amount * whole(shifted(zero, d)) for d in range(3)]
    two = squared(zero)
    for d in range(3):
        two = two + with_heat(zero, d)
    two = amount * two
    square = flow[0] * flow[0] + flow[1] * flow[1] + flow[2] * flow[2]
    momentum = [one[d] + flow[d] * none for d in range(3)]
    trace = (
        two
        + 2.0 * (flow[0] * one[0] + flow[1] * one[1] + flow[2] * one[2])
        + square * none
    )
    return [none] + momentum + [trace]


def kernel(
    digits,
    cells,
    state_ref,
    kind_hbm,
    boundary_ref,
    out_ref,
    macro_ref,
    kind_ref,
    table_ref,
    raw,
    h_first,
    h_second,
    moved,
    halo,
    acc,
    edge,
    edge_part,
    got_edge,
    edge_sum,
    part,
    got_a,
    mine,
    got_b,
    gathered,
    gauss,
    bend,
    tilt,
    keep_ref,
    input_sem,
    send_sem,
    recv_sem,
    edge_send,
    edge_recv,
    halo_send,
    halo_recv,
):
    points = RUN * digits
    vel = lax.axis_index("vel")
    cell = lax.axis_index("cell")
    jc = lax.rem(vel, digits)
    jb = lax.rem(vel // digits, digits)
    ja = vel // (digits * digits)
    lo = lax.rem(vel, 2)
    row = lax.rem(vel // 2, 8)
    col = vel // 16
    here = col * 2 + lax.rem(row, 2)
    there = (row // 2) * 2 + lo
    up = lax.rem(cell + 1, cells)
    down = lax.rem(cell + cells - 1, cells)

    def peer_a(other, slab):
        return ((other // 2) * 16 + (row // 2 * 2 + lax.rem(other, 2)) * 2 + lo, slab)

    def peer_b(other, slab):
        return (col * 16 + (other // 2 * 2 + lax.rem(row, 2)) * 2 + lax.rem(other, 2), slab)

    loads = [
        pltpu.make_async_copy(state_ref, raw, input_sem.at[0]),
        pltpu.make_async_copy(kind_hbm, kind_ref, input_sem.at[1]),
    ]
    barrier = pltpu.get_barrier_semaphore()
    greeted = [peer_a(lax.rem(here + k, 8), other) for k in range(8) for other in (up, down)]
    greeted += [peer_a(lax.rem(here + k, 8), cell) for k in range(1, 8)]
    greeted += [peer_b(lax.rem(there + k, 8), cell) for k in range(1, 8)]
    for device in greeted:
        pl.semaphore_signal(barrier, inc=1, device_id=device, device_id_type=MESH)
    for copy in loads:
        copy.start()
    for index, value in enumerate(one_dimensional_tables(points)):
        table_ref[index] = jnp.float32(value)

    lane = lax.broadcasted_iota(jnp.int32, (8, 128), 1)
    sub = lax.broadcasted_iota(jnp.int32, (8, 128), 0)
    in_z = lax.rem(lane, 32)
    z_first, z_last = in_z == 0, in_z == 31
    y_low, y_high = lane < 32, lane >= 96
    y_first, y_last = sub == 0, sub == 7
    has_down = jnp.where(cell > 0, 1.0, 0.0).astype(jnp.float32)
    has_up = jnp.where(cell < cells - 1, 1.0, 0.0).astype(jnp.float32)

    def speed(m, digit):
        return table_ref[4 * m + digit] if digits == 4 else table_ref[m]

    def weight(m, digit):
        return table_ref[points + 4 * m + digit] if digits == 4 else table_ref[points + m]

    def courant(m, digit):
        return table_ref[2 * points + 4 * m + digit] if digits == 4 else table_ref[2 * points + m]

    def run_sums(values):
        sums = None
        for mc, value in enumerate(values):
            sz = speed(mc, jc)
            terms = [weight(mc, jc) * value]
            for _ in range(3):
                terms.append(sz * terms[-1])
            sums = terms if sums is None else [x + y for x, y in zip(sums, terms)]
        return sums

    def add_run(total, values, mb):
        sy, w = speed(mb, jb), weight(mb, jb)
        result = []
        for n, term in enumerate(run_sums(values)):
            term = w * term
            row = [term]
            for _ in range(3 - n):
                term = sy * term
                row.append(term)
            if total is not None:
                row = [x + y for x, y in zip(total[n], row)]
            result.append(row)
        return result

    def add_moments(ref, place, total, ma, factor):
        sx = speed(ma, ja)
        w = weight(ma, ja) * factor
        wx, square = w * sx, sx * sx
        (z0, z0y, z0yy, z0yyy), (z1, z1y, z1yy), (z2, z2y), (z3,) = total
        rows = [
            w * z0,
            wx * z0,
            w * z0y,
            w * z1,
            (wx * sx) * z0,
            w * z0yy,
            w * z2,
            wx * z0y,
            wx * z1,
            w * z1y,
            wx * (square * z0 + (z0yy + z2)),
            w * (square * z0y + (z0yyy + z2y)),
            w * (square * z1 + (z1yy + z3)),
        ]
        for r in range(13):
            ref[r, place] += rows[r]

    def shift_y(value, positive):
        turned = pltpu.roll(value, 32 if positive else 96, 1)
        carried = pltpu.roll(turned, 1 if positive else 7, 0)
        edge_rows, lanes = (y_first, y_low) if positive else (y_last, y_high)
        return jnp.where(lanes, jnp.where(edge_rows, 0.0, carried), turned)

    def shift_z(value, positive):
        turned = pltpu.roll(value, 1 if positive else 127, 1)
        return jnp.where(z_first if positive else z_last, 0.0, turned)

    def relaxed(i, ma, mb, plane, pi, outer):
        base = gauss[ma, plane] * gauss[RUN + mb, plane]
        bend_xy = bend[ma, plane] + bend[RUN + mb, plane]
        tilt_xy = tilt[ma, plane] + tilt[RUN + mb, plane]
        keep = keep_ref[plane]
        values = []
        if outer:
            kx = courant(ma, ja) * jnp.where(pi == 1, has_down, has_up)
        for mc in range(RUN):
            node = i * RUN + mc
            value = moved[plane, node]
            if outer:
                value = value + kx * halo[outer - 1, pi, node - pi * HALF]
            t = (tilt_xy + tilt[2 * RUN + mc, plane]) * (bend_xy + bend[2 * RUN + mc, plane])
            values.append(keep * value + (base * gauss[2 * RUN + mc, plane]) * (1.0 + t))
        return values

    def new_plane(step, i, ma, mb, plane, pi, outer):
        if step == 0:
            return [
                raw[pl.ds((i * RUN + mc) * 16 + plane, 8, stride=2), :] for mc in range(RUN)
            ]
        return relaxed(i, ma, mb, plane, pi, step if outer else 0)

    def send_edges(step, held):
        copies = []
        for r in range(13):
            for pi in range(2):
                edge_part[step, pi, pl.ds(r, 8, stride=16), :] = edge[pi, r]
        for k in ORDER + (0,):
            other = lax.rem(here + k, 8)
            for pi, slab in ((1, up), (0, down)):
                copies.append(
                    pltpu.make_async_remote_copy(
                        src_ref=edge_part.at[step, pi, pl.ds(pl.multiple_of(other * 16, 16), 13)],
                        dst_ref=got_edge.at[step, pi, here],
                        send_sem=edge_send.at[step, pi, k],
                        recv_sem=edge_recv.at[step, pi, k],
                        device_id=peer_a(other, slab),
                        device_id_type=MESH,
                    )
                )
        for part_index, (first, count) in enumerate(((0, EARLY), (EARLY, HALF - EARLY))):
            for pi, other in ((1, up), (0, down)):
                copies.append(
                    pltpu.make_async_remote_copy(
                        src_ref=held.at[pl.ds(pi * HALF + first, count)],
                        dst_ref=halo.at[step, pi, pl.ds(first, count)],
                        send_sem=halo_send.at[step, part_index, pi],
                        recv_sem=halo_recv.at[step, part_index, pi],
                        device_id=(vel, other),
                        device_id_type=MESH,
                    )
                )
        for copy in copies[:18]:
            copy.start()
        return copies[:16], copies[16:]

    def exchange(step, phase, source, target, index, peer):
        copies = []
        for k in ORDER:
            other = lax.rem(index + k, 8)
            copy = pltpu.make_async_remote_copy(
                src_ref=source(other),
                dst_ref=target,
                send_sem=send_sem.at[step, phase, k - 1],
                recv_sem=recv_sem.at[step, phase, k - 1],
                device_id=peer(other, cell),
                device_id_type=MESH,
            )
            copy.start()
            copies.append(copy)
        return copies

    def slice_rows(index, count):
        return pl.ds(pl.multiple_of(index * ROWS, ROWS), count)

    def parameters_of(step, index, total_ref):
        moment = [total_ref[pl.ds(r, 2, stride=13), :] for r in range(13)]
        kind = kind_ref[pl.ds(2 * index, 2), :]
        boundary = [boundary_ref[r] for r in range(6)]
        rows = step_parameters(moment, kind, boundary)
        for r in range(9 if step < STEPS - 1 else 14):
            gathered[step, pl.ds(index * ROWS + 2 * r, 2), :] = rows[r]

    def all_sums(step, edges, late):
        for r in range(13):
            for p in range(2):
                part[step, pl.ds(13 * p + r, 8, stride=ROWS), :] = acc[r, p]
        copies = exchange(
            step, 0, lambda other: part.at[step, slice_rows(other, USED)], got_a.at[step, here], here, peer_a
        )
        got_a[step, here] = part[step, slice_rows(here, USED), :]
        for copy in edges:
            copy.wait()
        for p in range(2):
            from_edge = got_edge[step, 1 - p, 0]
            for k in range(1, 8):
                from_edge = from_edge + got_edge[step, 1 - p, k]
            edge_sum[pl.ds(13 * p, 13), :] = from_edge * (has_down if p == 0 else has_up)
        for copy in copies:
            copy.wait()
        total = edge_sum[...]
        for k in range(8):
            total = total + got_a[step, k]
        mine[step] = total
        copies = exchange(
            step, 1, lambda other: mine.at[step], got_b.at[step, there], there, peer_b
        )
        got_b[step, there] = total
        for copy in copies:
            copy.wait()
        for copy in late:
            copy.start()
        total = got_b[step, 0]
        for k in range(1, 8):
            total = total + got_b[step, k]
        acc_rows = got_b.at[step, there]
        acc_rows[...] = total
        parameters_of(step, here, acc_rows)
        block = gathered.at[step, slice_rows(here, 18 if step < STEPS - 1 else 28)]
        copies = exchange(step, 2, lambda other: block, block, here, peer_a)
        for copy in copies:
            copy.wait()

    def gathered_rows(step, r):
        return [gathered[step, pl.ds(2 * r + p, 8, stride=ROWS), :] for p in range(2)]

    def build_tables(step):
        keep, amount, *rest = [gathered_rows(step, r) for r in range(9)]
        for p in range(2):
            keep_ref[p] = keep[p]

        def fill(m, carry):
            for d, digit in enumerate((ja, jb, jc)):
                s = speed(m, digit)
                for p in range(2):
                    c = s - rest[d][p]
                    inverse = rest[3][p]
                    scaled = c * c * inverse
                    value = jnp.exp(-scaled)
                    lift = scaled + scaled
                    if d == 0:
                        value = value * amount[p]
                        lift = lift - 5.0
                    gauss[d * RUN + m, p] = value
                    bend[d * RUN + m, p] = lift
                    tilt[d * RUN + m, p] = c * rest[4 + d][p]
            return carry

        lax.fori_loop(0, RUN, fill, 0)

    for copy in loads:
        copy.wait()
    for step in range(STEPS):
        held = h_first if step == 0 else h_second
        edge[...] = jnp.zeros(edge.shape, jnp.float32)
        acc[...] = jnp.zeros(acc.shape, jnp.float32)

        def inner(ma, carry, step=step, held=held):
            pi = ma // (RUN // 2)
            total = None
            for mb in range(RUN):
                i = ma * RUN + mb
                values = new_plane(step, i, ma, mb, pi, pi, False)
                for mc in range(RUN):
                    held[i * RUN + mc] = values[mc]
                total = add_run(total, values, mb)
            add_moments(edge.at[pi], slice(None), total, ma, courant(ma, ja))
            return carry

        lax.fori_loop(0, RUN, inner, 0)
        if step == 0:
            pl.semaphore_wait(barrier, len(greeted))
        edges, halos = send_edges(step, held)
        if step > 0:
            for copy in halos_before:
                copy.wait()

        for half in range(2):

            def transport(ma, carry, half=half, step=step, held=held):
                pi = ma // (RUN // 2)
                kx = courant(ma, ja)
                inner_total, outer_total = None, None
                for mb in range(half * (RUN // 2), (half + 1) * (RUN // 2)):
                    i = ma * RUN + mb
                    ky = courant(mb, jb)
                    at_inner, at_outer = [], []
                    values = new_plane(step, i, ma, mb, 1 - pi, pi, True)
                    for mc in range(RUN):
                        node = i * RUN + mc
                        kz = courant(mc, jc)
                        stay = 1.0 - (kx + ky + kz)
                        near, far = held[node], values[mc]

                        def flat(value):
                            return (
                                stay * value
                                + ky * shift_y(value, half == 1)
                                + kz * shift_z(value, mc >= RUN // 2)
                            )

                        at_inner.append(flat(near) + kx * far)
                        at_outer.append(flat(far))
                        moved[pi, node] = at_inner[-1]
                        moved[1 - pi, node] = at_outer[-1]
                    inner_total = add_run(inner_total, at_inner, mb)
                    outer_total = add_run(outer_total, at_outer, mb)
                add_moments(acc, pi, inner_total, ma, 1.0)
                add_moments(acc, 1 - pi, outer_total, ma, 1.0)
                return carry

            lax.fori_loop(0, RUN, transport, 0, unroll=2)
        all_sums(step, edges, halos[2:])
        build_tables(step)
        halos_before = halos

    for copy in halos_before:
        copy.wait()

    def last(i, carry):
        ma, mb = i // RUN, lax.rem(i, RUN)
        pi = ma // (RUN // 2)
        for plane, is_outer in ((pi, 0), (1 - pi, STEPS)):
            values = relaxed(i, ma, mb, plane, pi, is_outer)
            for mc in range(RUN):
                out_ref[pl.ds((i * RUN + mc) * 16 + plane, 8, stride=2), :] = values[mc]
        return carry

    lax.fori_loop(0, PAIRS, last, 0, unroll=3)

    final = STEPS - 1
    for p in range(2):
        keep, amount, ux, uy, uz, inverse, qx, qy, qz, *old = [
            gathered_rows(final, r)[p] for r in range(14)
        ]
        flow, heat = (ux, uy, uz), (qx, qy, qz)

        def sums(a, carry):
            s, w = table_ref[a], table_ref[points + a]
            result = []
            for d in range(3):
                c = s - flow[d]
                term = w * jnp.exp(-(c * c * inverse))
                for n in range(6):
                    result.append(carry[d * 6 + n] + term)
                    term = term * c
            return tuple(result)

        power = lax.fori_loop(
            0, points, sums, tuple(jnp.zeros((8, 128), jnp.float32) for _ in range(18)), unroll=4
        )
        power = [power[d * 6 : d * 6 + 6] for d in range(3)]
        added = added_moments(power, amount, flow, inverse, heat)
        density, mx, my, mz, trace = [keep * x + y for x, y in zip(old, added)]
        u = [mx / density, my / density, mz / density]
        square = u[0] * u[0] + u[1] * u[1] + u[2] * u[2]
        result = [density] + u + [(trace / density - square) / 3.0]
        for r in range(5):
            macro_ref[pl.ds(r * 16 + p, 8, stride=2), :] = result[r]


def interleaved(array):
    lead = array.shape[:-2]
    return array.reshape(lead + (2, 8, 128)).swapaxes(-3, -2).reshape(-1, 128)


def restored(array, lead):
    return array.reshape((lead, 8, 2, 128)).swapaxes(1, 2).reshape(lead, 2, 1024)


def shards(digits, cells, state_init, cell_kind, boundary_state):
    vmem = functools.partial(pl.BlockSpec, memory_space=pltpu.VMEM)
    smem = functools.partial(pl.BlockSpec, memory_space=pltpu.SMEM)
    f32 = jnp.float32
    state, macro = pl.pallas_call(
        functools.partial(kernel, digits, cells),
        out_shape=(
            jax.ShapeDtypeStruct((NODES * 16, 128), f32),
            jax.ShapeDtypeStruct((80, 128), f32),
        ),
        in_specs=[pl.BlockSpec(memory_space=pltpu.HBM), pl.BlockSpec(memory_space=pltpu.HBM), smem()],
        out_specs=(vmem(), vmem()),
        scratch_shapes=[
            pltpu.VMEM((16, 128), jnp.int32),
            pltpu.SMEM((3 * RUN * digits,), f32),
            pltpu.VMEM((NODES * 16, 128), f32),
            pltpu.VMEM((NODES, 8, 128), f32),
            pltpu.VMEM((NODES, 8, 128), f32),
            pltpu.VMEM((2, NODES, 8, 128), f32),
            pltpu.VMEM((STEPS, 2, HALF, 8, 128), f32),
            pltpu.VMEM((13, 2, 8, 128), f32),
            pltpu.VMEM((2, 13, 8, 128), f32),
            pltpu.VMEM((STEPS, 2, 8 * 16, 128), f32),
            pltpu.VMEM((STEPS, 2, 8, 13, 128), f32),
            pltpu.VMEM((USED, 128), f32),
            pltpu.VMEM((STEPS, 8 * ROWS, 128), f32),
            pltpu.VMEM((STEPS, 8, USED, 128), f32),
            pltpu.VMEM((STEPS, USED, 128), f32),
            pltpu.VMEM((STEPS, 8, USED, 128), f32),
            pltpu.VMEM((STEPS, 8 * ROWS, 128), f32),
            pltpu.VMEM((3 * RUN, 2, 8, 128), f32),
            pltpu.VMEM((3 * RUN, 2, 8, 128), f32),
            pltpu.VMEM((3 * RUN, 2, 8, 128), f32),
            pltpu.VMEM((2, 8, 128), f32),
            pltpu.SemaphoreType.DMA((2,)),
            pltpu.SemaphoreType.DMA((STEPS, 3, 7)),
            pltpu.SemaphoreType.DMA((STEPS, 3, 7)),
            pltpu.SemaphoreType.DMA((STEPS, 2, 8)),
            pltpu.SemaphoreType.DMA((STEPS, 2, 8)),
            pltpu.SemaphoreType.DMA((STEPS, 2, 2)),
            pltpu.SemaphoreType.DMA((STEPS, 2, 2)),
        ],
        compiler_params=pltpu.CompilerParams(
            collective_id=0, has_side_effects=True, vmem_limit_bytes=52 * 1024 * 1024
        ),
    )(interleaved(state_init), interleaved(cell_kind), boundary_state)
    return restored(state, NODES), restored(macro, 5)


def solution(mesh):
    in_specs = (P("vel", "cell", None), P("cell", None), P())
    out_specs = (P("vel", "cell", None), P(None, "cell", None))
    body = functools.partial(shards, 4, 8)
    return jax.shard_map(body, mesh=mesh, in_specs=in_specs, out_specs=out_specs, check_vma=False)
```

```python
import functools

import jax
import jax.numpy as jnp
import numpy as np
from jax import lax
from jax.experimental import pallas as pl
from jax.experimental.pallas import tpu as pltpu
from jax.sharding import PartitionSpec as P

QUAD_ABSCISSAE = 24
RUN = 6
STEPS = 2


MOMENTUM_RATIO = 2.0 / 3.0
SHEAR_EXPONENT = 0.81
SHEAR_REFERENCE = 0.05
TIME_INCREMENT = 0.03125

NODES = RUN * RUN * RUN
HALF = NODES // 2
EARLY = 88
PAIRS = RUN * RUN
USED = 26
ROWS = 32
ORDER = (4, 3, 5, 2, 6, 1, 7)
MESH = pl.DeviceIdType.MESH


def hermite_rule(points):
    start_value = np.pi ** (-0.25)
    node_list = np.zeros(points)
    weight_list = np.zeros(points)
    guess_root = 0.0
    slope_value = 1.0
    for index in range((points + 1) // 2):
        if index == 0:
            guess_root = np.sqrt(2.0 * points + 1.0) - 1.85575 * (2.0 * points + 1.0) ** (-0.16667)
        elif index == 1:
            guess_root = guess_root - 1.14 * points**0.426 / guess_root
        elif index == 2:
            guess_root = 1.86 * guess_root - 0.86 * node_list[0]
        elif index == 3:
            guess_root = 1.91 * guess_root - 0.91 * node_list[1]
        else:
            guess_root = 2.0 * guess_root - node_list[index - 2]
        for sweep in range(60):
            poly_now = start_value
            poly_prev = 0.0
            for degree in range(points):
                poly_old = poly_prev
                poly_prev = poly_now
                poly_now = (
                    guess_root * np.sqrt(2.0 / (degree + 1)) * poly_prev
                    - np.sqrt(degree / (degree + 1.0)) * poly_old
                )
            slope_value = np.sqrt(2.0 * points) * poly_prev
            guess_root = guess_root - poly_now / slope_value
        node_list[index] = guess_root
        node_list[points - 1 - index] = -guess_root
        weight_list[index] = 2.0 / (slope_value * slope_value)
        weight_list[points - 1 - index] = weight_list[index]
    return (node_list[::-1].copy(), weight_list[::-1].copy())


def one_dimensional_tables(points):
    abscissa, weights = hermite_rule(points)
    speed = np.sqrt(2.0) * abscissa
    weight = weights * np.exp(abscissa * abscissa) / np.sqrt(np.pi)
    return np.concatenate([speed, weight, TIME_INCREMENT * np.abs(speed)])


def step_parameters(moment, kind, boundary):
    density = moment[0]
    first = moment[1:4]
    flow = [value / density for value in first]
    trace = moment[4] + moment[5] + moment[6]
    square = flow[0] * flow[0] + flow[1] * flow[1] + flow[2] * flow[2]
    temperature = (trace / density - square) / 3.0
    along = flow[0] * first[0] + flow[1] * first[1] + flow[2] * first[2]
    pairs = ((4, 7, 8), (7, 5, 9), (8, 9, 6))
    heat = []
    for d in range(3):
        tensor = (
            moment[pairs[d][0]] * flow[0]
            + moment[pairs[d][1]] * flow[1]
            + moment[pairs[d][2]] * flow[2]
        )
        heat.append(
            0.5
            * (
                moment[10 + d]
                - 2.0 * tensor
                + square * first[d]
                - flow[d] * trace
                + 2.0 * flow[d] * along
                - flow[d] * square * density
            )
        )
    pressure = density * temperature
    rate = (
        TIME_INCREMENT
        * pressure
        / (SHEAR_REFERENCE * jnp.exp(SHEAR_EXPONENT * jnp.log(temperature)))
    )
    keep = 1.0 / (1.0 + rate)
    scale = (1.0 - MOMENTUM_RATIO) / (5.0 * pressure * temperature)

    def pick(fluid, wall, inlet, outlet):
        return jnp.where(
            kind == 0, fluid, jnp.where(kind == 1, wall, jnp.where(kind == 2, inlet, outlet))
        )

    level = pick(temperature, boundary[5], boundary[4], 1.0)
    amount = pick(density * rate * keep, density, boundary[0], 0.0)
    return (
        [pick(keep, 0.0, 0.0, 1.0), amount / (level * jnp.sqrt(level))]
        + [pick(flow[d], 0.0, boundary[1 + d], 0.0) for d in range(3)]
        + [0.5 / level]
        + [pick(heat[d] * scale, 0.0, 0.0, 0.0) for d in range(3)]
        + [density, first[0], first[1], first[2], trace]
    )


def added_moments(power, amount, flow, inverse, heat):
    planes = {}

    def product(i, j, k):
        if (i, j) not in planes:
            planes[i, j] = power[0][i] * power[1][j]
        return planes[i, j] * power[2][k]

    def shifted(base, d, n=1):
        return tuple(base[e] + (n if e == d else 0) for e in range(3))

    def squared(base):
        return product(*shifted(base, 0, 2)) + product(*shifted(base, 1, 2)) + product(*shifted(base, 2, 2))

    double = inverse + inverse

    def whole(base):
        total = product(*base)
        for d in range(3):
            with_d = shifted(base, d)
            total = total + heat[d] * (double * squared(with_d) - 5.0 * product(*with_d))
        return total

    def with_heat(base, d):
        at = shifted(base, d)
        fourth = None
        for e in range(3):
            for f in range(3):
                term = product(*shifted(shifted(at, e, 2), f, 2))
                fourth = term if fourth is None else fourth + term
        return heat[d] * (double * fourth - 5.0 * squared(at))

    zero = (0, 0, 0)
    none = amount * whole(zero)
    one = [amount * whole(shifted(zero, d)) for d in range(3)]
    two = squared(zero)
    for d in range(3):
        two = two + with_heat(zero, d)
    two = amount * two
    square = flow[0] * flow[0] + flow[1] * flow[1] + flow[2] * flow[2]
    momentum = [one[d] + flow[d] * none for d in range(3)]
    trace = (
        two
        + 2.0 * (flow[0] * one[0] + flow[1] * one[1] + flow[2] * one[2])
        + square * none
    )
    return [none] + momentum + [trace]


def kernel(
    digits,
    cells,
    state_ref,
    kind_hbm,
    boundary_ref,
    out_ref,
    macro_ref,
    kind_ref,
    table_ref,
    raw,
    h_first,
    h_second,
    moved,
    halo,
    acc,
    edge,
    edge_part,
    got_edge,
    edge_sum,
    part,
    got_a,
    mine,
    got_b,
    gathered,
    gauss,
    bend,
    tilt,
    keep_ref,
    input_sem,
    send_sem,
    recv_sem,
    edge_send,
    edge_recv,
    halo_send,
    halo_recv,
):
    points = RUN * digits
    vel = lax.axis_index("vel")
    cell = lax.axis_index("cell")
    jc = lax.rem(vel, digits)
    jb = lax.rem(vel // digits, digits)
    ja = vel // (digits * digits)
    lo = lax.rem(vel, 2)
    row = lax.rem(vel // 2, 8)
    col = vel // 16
    here = col * 2 + lax.rem(row, 2)
    there = (row // 2) * 2 + lo
    up = lax.rem(cell + 1, cells)
    down = lax.rem(cell + cells - 1, cells)

    def peer_a(other, slab):
        return ((other // 2) * 16 + (row // 2 * 2 + lax.rem(other, 2)) * 2 + lo, slab)

    def peer_b(other, slab):
        return (col * 16 + (other // 2 * 2 + lax.rem(row, 2)) * 2 + lax.rem(other, 2), slab)

    loads = [
        pltpu.make_async_copy(state_ref, raw, input_sem.at[0]),
        pltpu.make_async_copy(kind_hbm, kind_ref, input_sem.at[1]),
    ]
    barrier = pltpu.get_barrier_semaphore()
    greeted = [peer_a(lax.rem(here + k, 8), other) for k in range(8) for other in (up, down)]
    greeted += [peer_a(lax.rem(here + k, 8), cell) for k in range(1, 8)]
    greeted += [peer_b(lax.rem(there + k, 8), cell) for k in range(1, 8)]
    for device in greeted:
        pl.semaphore_signal(barrier, inc=1, device_id=device, device_id_type=MESH)
    for copy in loads:
        copy.start()
    for index, value in enumerate(one_dimensional_tables(points)):
        table_ref[index] = jnp.float32(value)

    lane = lax.broadcasted_iota(jnp.int32, (8, 128), 1)
    sub = lax.broadcasted_iota(jnp.int32, (8, 128), 0)
    in_z = lax.rem(lane, 32)
    z_first, z_last = in_z == 0, in_z == 31
    y_low, y_high = lane < 32, lane >= 96
    y_first, y_last = sub == 0, sub == 7
    has_down = jnp.where(cell > 0, 1.0, 0.0).astype(jnp.float32)
    has_up = jnp.where(cell < cells - 1, 1.0, 0.0).astype(jnp.float32)

    def speed(m, digit):
        return table_ref[4 * m + digit] if digits == 4 else table_ref[m]

    def weight(m, digit):
        return table_ref[points + 4 * m + digit] if digits == 4 else table_ref[points + m]

    def courant(m, digit):
        return table_ref[2 * points + 4 * m + digit] if digits == 4 else table_ref[2 * points + m]

    def run_sums(values):
        sums = None
        for mc, value in enumerate(values):
            sz = speed(mc, jc)
            terms = [weight(mc, jc) * value]
            for _ in range(3):
                terms.append(sz * terms[-1])
            sums = terms if sums is None else [x + y for x, y in zip(sums, terms)]
        return sums

    def add_run(total, values, mb):
        sy, w = speed(mb, jb), weight(mb, jb)
        result = []
        for n, term in enumerate(run_sums(values)):
            term = w * term
            row = [term]
            for _ in range(3 - n):
                term = sy * term
                row.append(term)
            if total is not None:
                row = [x + y for x, y in zip(total[n], row)]
            result.append(row)
        return result

    def add_moments(ref, place, total, ma, factor):
        sx = speed(ma, ja)
        w = weight(ma, ja) * factor
        wx, square = w * sx, sx * sx
        (z0, z0y, z0yy, z0yyy), (z1, z1y, z1yy), (z2, z2y), (z3,) = total
        rows = [
            w * z0,
            wx * z0,
            w * z0y,
            w * z1,
            (wx * sx) * z0,
            w * z0yy,
            w * z2,
            wx * z0y,
            wx * z1,
            w * z1y,
            wx * (square * z0 + (z0yy + z2)),
            w * (square * z0y + (z0yyy + z2y)),
            w * (square * z1 + (z1yy + z3)),
        ]
        for r in range(13):
            ref[r, place] += rows[r]

    def shift_y(value, positive):
        turned = pltpu.roll(value, 32 if positive else 96, 1)
        carried = pltpu.roll(turned, 1 if positive else 7, 0)
        edge_rows, lanes = (y_first, y_low) if positive else (y_last, y_high)
        return jnp.where(lanes, jnp.where(edge_rows, 0.0, carried), turned)

    def shift_z(value, positive):
        turned = pltpu.roll(value, 1 if positive else 127, 1)
        return jnp.where(z_first if positive else z_last, 0.0, turned)

    def relaxed(i, ma, mb, plane, pi, outer):
        base = gauss[ma, plane] * gauss[RUN + mb, plane]
        bend_xy = bend[ma, plane] + bend[RUN + mb, plane]
        tilt_xy = tilt[ma, plane] + tilt[RUN + mb, plane]
        keep = keep_ref[plane]
        values = []
        if outer:
            kx = courant(ma, ja) * jnp.where(pi == 1, has_down, has_up)
        for mc in range(RUN):
            node = i * RUN + mc
            value = moved[plane, node]
            if outer:
                value = value + kx * halo[outer - 1, pi, node - pi * HALF]
            t = (tilt_xy + tilt[2 * RUN + mc, plane]) * (bend_xy + bend[2 * RUN + mc, plane])
            values.append(keep * value + (base * gauss[2 * RUN + mc, plane]) * (1.0 + t))
        return values

    def new_plane(step, i, ma, mb, plane, pi, outer):
        if step == 0:
            return [
                raw[pl.ds((i * RUN + mc) * 16 + plane, 8, stride=2), :] for mc in range(RUN)
            ]
        return relaxed(i, ma, mb, plane, pi, step if outer else 0)

    def send_edges(step, held):
        copies = []
        for r in range(13):
            for pi in range(2):
                edge_part[step, pi, pl.ds(r, 8, stride=16), :] = edge[pi, r]
        for k in ORDER + (0,):
            other = lax.rem(here + k, 8)
            for pi, slab in ((1, up), (0, down)):
                copies.append(
                    pltpu.make_async_remote_copy(
                        src_ref=edge_part.at[step, pi, pl.ds(pl.multiple_of(other * 16, 16), 13)],
                        dst_ref=got_edge.at[step, pi, here],
                        send_sem=edge_send.at[step, pi, k],
                        recv_sem=edge_recv.at[step, pi, k],
                        device_id=peer_a(other, slab),
                        device_id_type=MESH,
                    )
                )
        for part_index, (first, count) in enumerate(((0, EARLY), (EARLY, HALF - EARLY))):
            for pi, other in ((1, up), (0, down)):
                copies.append(
                    pltpu.make_async_remote_copy(
                        src_ref=held.at[pl.ds(pi * HALF + first, count)],
                        dst_ref=halo.at[step, pi, pl.ds(first, count)],
                        send_sem=halo_send.at[step, part_index, pi],
                        recv_sem=halo_recv.at[step, part_index, pi],
                        device_id=(vel, other),
                        device_id_type=MESH,
                    )
                )
        for copy in copies[:18]:
            copy.start()
        return copies[:16], copies[16:]

    def exchange(step, phase, source, target, index, peer):
        copies = []
        for k in ORDER:
            other = lax.rem(index + k, 8)
            copy = pltpu.make_async_remote_copy(
                src_ref=source(other),
                dst_ref=target,
                send_sem=send_sem.at[step, phase, k - 1],
                recv_sem=recv_sem.at[step, phase, k - 1],
                device_id=peer(other, cell),
                device_id_type=MESH,
            )
            copy.start()
            copies.append(copy)
        return copies

    def slice_rows(index, count):
        return pl.ds(pl.multiple_of(index * ROWS, ROWS), count)

    def parameters_of(step, index, total_ref):
        moment = [total_ref[pl.ds(r, 2, stride=13), :] for r in range(13)]
        kind = kind_ref[pl.ds(2 * index, 2), :]
        boundary = [boundary_ref[r] for r in range(6)]
        rows = step_parameters(moment, kind, boundary)
        for r in range(9 if step < STEPS - 1 else 14):
            gathered[step, pl.ds(index * ROWS + 2 * r, 2), :] = rows[r]

    def all_sums(step, edges, late):
        for r in range(13):
            for p in range(2):
                part[step, pl.ds(13 * p + r, 8, stride=ROWS), :] = acc[r, p]
        copies = exchange(
            step, 0, lambda other: part.at[step, slice_rows(other, USED)], got_a.at[step, here], here, peer_a
        )
        got_a[step, here] = part[step, slice_rows(here, USED), :]
        for copy in edges:
            copy.wait()
        for p in range(2):
            from_edge = got_edge[step, 1 - p, 0]
            for k in range(1, 8):
                from_edge = from_edge + got_edge[step, 1 - p, k]
            edge_sum[pl.ds(13 * p, 13), :] = from_edge * (has_down if p == 0 else has_up)
        for copy in copies:
            copy.wait()
        total = edge_sum[...]
        for k in range(8):
            total = total + got_a[step, k]
        mine[step] = total
        copies = exchange(
            step, 1, lambda other: mine.at[step], got_b.at[step, there], there, peer_b
        )
        got_b[step, there] = total
        for copy in copies:
            copy.wait()
        for copy in late:
            copy.start()
        total = got_b[step, 0]
        for k in range(1, 8):
            total = total + got_b[step, k]
        acc_rows = got_b.at[step, there]
        acc_rows[...] = total
        parameters_of(step, here, acc_rows)
        block = gathered.at[step, slice_rows(here, 18 if step < STEPS - 1 else 28)]
        copies = exchange(step, 2, lambda other: block, block, here, peer_a)
        for copy in copies:
            copy.wait()

    def gathered_rows(step, r):
        return [gathered[step, pl.ds(2 * r + p, 8, stride=ROWS), :] for p in range(2)]

    def build_tables(step):
        keep, amount, *rest = [gathered_rows(step, r) for r in range(9)]
        for p in range(2):
            keep_ref[p] = keep[p]

        def fill(m, carry):
            for d, digit in enumerate((ja, jb, jc)):
                s = speed(m, digit)
                for p in range(2):
                    c = s - rest[d][p]
                    inverse = rest[3][p]
                    scaled = c * c * inverse
                    value = jnp.exp(-scaled)
                    lift = scaled + scaled
                    if d == 0:
                        value = value * amount[p]
                        lift = lift - 5.0
                    gauss[d * RUN + m, p] = value
                    bend[d * RUN + m, p] = lift
                    tilt[d * RUN + m, p] = c * rest[4 + d][p]
            return carry

        lax.fori_loop(0, RUN, fill, 0)

    for copy in loads:
        copy.wait()
    for step in range(STEPS):
        held = h_first if step == 0 else h_second
        edge[...] = jnp.zeros(edge.shape, jnp.float32)
        acc[...] = jnp.zeros(acc.shape, jnp.float32)

        def inner(ma, carry, step=step, held=held):
            pi = ma // (RUN // 2)
            total = None
            for mb in range(RUN):
                i = ma * RUN + mb
                values = new_plane(step, i, ma, mb, pi, pi, False)
                for mc in range(RUN):
                    held[i * RUN + mc] = values[mc]
                total = add_run(total, values, mb)
            add_moments(edge.at[pi], slice(None), total, ma, courant(ma, ja))
            return carry

        lax.fori_loop(0, RUN, inner, 0)
        if step == 0:
            pl.semaphore_wait(barrier, len(greeted))
        edges, halos = send_edges(step, held)
        if step > 0:
            for copy in halos_before:
                copy.wait()

        for half in range(2):

            def transport(ma, carry, half=half, step=step, held=held):
                pi = ma // (RUN // 2)
                kx = courant(ma, ja)
                inner_total, outer_total = None, None
                for mb in range(half * (RUN // 2), (half + 1) * (RUN // 2)):
                    i = ma * RUN + mb
                    ky = courant(mb, jb)
                    at_inner, at_outer = [], []
                    values = new_plane(step, i, ma, mb, 1 - pi, pi, True)
                    for mc in range(RUN):
                        node = i * RUN + mc
                        kz = courant(mc, jc)
                        stay = 1.0 - (kx + ky + kz)
                        near, far = held[node], values[mc]

                        def flat(value):
                            return (
                                stay * value
                                + ky * shift_y(value, half == 1)
                                + kz * shift_z(value, mc >= RUN // 2)
                            )

                        at_inner.append(flat(near) + kx * far)
                        at_outer.append(flat(far))
                        moved[pi, node] = at_inner[-1]
                        moved[1 - pi, node] = at_outer[-1]
                    inner_total = add_run(inner_total, at_inner, mb)
                    outer_total = add_run(outer_total, at_outer, mb)
                add_moments(acc, pi, inner_total, ma, 1.0)
                add_moments(acc, 1 - pi, outer_total, ma, 1.0)
                return carry

            lax.fori_loop(0, RUN, transport, 0, unroll=2)
        all_sums(step, edges, halos[2:])
        build_tables(step)
        halos_before = halos

    final = STEPS - 1
    for p in range(2):
        keep, amount, ux, uy, uz, inverse, qx, qy, qz, *old = [
            gathered_rows(final, r)[p] for r in range(14)
        ]
        flow, heat = (ux, uy, uz), (qx, qy, qz)

        def sums(a, carry):
            s, w = table_ref[a], table_ref[points + a]
            result = []
            for d in range(3):
                c = s - flow[d]
                term = w * jnp.exp(-(c * c * inverse))
                for n in range(6):
                    result.append(carry[d * 6 + n] + term)
                    term = term * c
            return tuple(result)

        power = lax.fori_loop(
            0, points, sums, tuple(jnp.zeros((8, 128), jnp.float32) for _ in range(18)), unroll=4
        )
        power = [power[d * 6 : d * 6 + 6] for d in range(3)]
        added = added_moments(power, amount, flow, inverse, heat)
        density, mx, my, mz, trace = [keep * x + y for x, y in zip(old, added)]
        u = [mx / density, my / density, mz / density]
        square = u[0] * u[0] + u[1] * u[1] + u[2] * u[2]
        result = [density] + u + [(trace / density - square) / 3.0]
        for r in range(5):
            macro_ref[pl.ds(r * 16 + p, 8, stride=2), :] = result[r]

    for copy in halos_before:
        copy.wait()

    def last(i, carry):
        ma, mb = i // RUN, lax.rem(i, RUN)
        pi = ma // (RUN // 2)
        for plane, is_outer in ((pi, 0), (1 - pi, STEPS)):
            values = relaxed(i, ma, mb, plane, pi, is_outer)
            for mc in range(RUN):
                out_ref[pl.ds((i * RUN + mc) * 16 + plane, 8, stride=2), :] = values[mc]
        return carry

    lax.fori_loop(0, PAIRS, last, 0, unroll=3)


def interleaved(array):
    lead = array.shape[:-2]
    return array.reshape(lead + (2, 8, 128)).swapaxes(-3, -2).reshape(-1, 128)


def restored(array, lead):
    return array.reshape((lead, 8, 2, 128)).swapaxes(1, 2).reshape(lead, 2, 1024)


def shards(digits, cells, state_init, cell_kind, boundary_state):
    vmem = functools.partial(pl.BlockSpec, memory_space=pltpu.VMEM)
    smem = functools.partial(pl.BlockSpec, memory_space=pltpu.SMEM)
    f32 = jnp.float32
    state, macro = pl.pallas_call(
        functools.partial(kernel, digits, cells),
        out_shape=(
            jax.ShapeDtypeStruct((NODES * 16, 128), f32),
            jax.ShapeDtypeStruct((80, 128), f32),
        ),
        in_specs=[pl.BlockSpec(memory_space=pltpu.HBM), pl.BlockSpec(memory_space=pltpu.HBM), smem()],
        out_specs=(vmem(), vmem()),
        scratch_shapes=[
            pltpu.VMEM((16, 128), jnp.int32),
            pltpu.SMEM((3 * RUN * digits,), f32),
            pltpu.VMEM((NODES * 16, 128), f32),
            pltpu.VMEM((NODES, 8, 128), f32),
            pltpu.VMEM((NODES, 8, 128), f32),
            pltpu.VMEM((2, NODES, 8, 128), f32),
            pltpu.VMEM((STEPS, 2, HALF, 8, 128), f32),
            pltpu.VMEM((13, 2, 8, 128), f32),
            pltpu.VMEM((2, 13, 8, 128), f32),
            pltpu.VMEM((STEPS, 2, 8 * 16, 128), f32),
            pltpu.VMEM((STEPS, 2, 8, 13, 128), f32),
            pltpu.VMEM((USED, 128), f32),
            pltpu.VMEM((STEPS, 8 * ROWS, 128), f32),
            pltpu.VMEM((STEPS, 8, USED, 128), f32),
            pltpu.VMEM((STEPS, USED, 128), f32),
            pltpu.VMEM((STEPS, 8, USED, 128), f32),
            pltpu.VMEM((STEPS, 8 * ROWS, 128), f32),
            pltpu.VMEM((3 * RUN, 2, 8, 128), f32),
            pltpu.VMEM((3 * RUN, 2, 8, 128), f32),
            pltpu.VMEM((3 * RUN, 2, 8, 128), f32),
            pltpu.VMEM((2, 8, 128), f32),
            pltpu.SemaphoreType.DMA((2,)),
            pltpu.SemaphoreType.DMA((STEPS, 3, 7)),
            pltpu.SemaphoreType.DMA((STEPS, 3, 7)),
            pltpu.SemaphoreType.DMA((STEPS, 2, 8)),
            pltpu.SemaphoreType.DMA((STEPS, 2, 8)),
            pltpu.SemaphoreType.DMA((STEPS, 2, 2)),
            pltpu.SemaphoreType.DMA((STEPS, 2, 2)),
        ],
        compiler_params=pltpu.CompilerParams(
            collective_id=0, has_side_effects=True, vmem_limit_bytes=52 * 1024 * 1024
        ),
    )(interleaved(state_init), interleaved(cell_kind), boundary_state)
    return restored(state, NODES), restored(macro, 5)


def solution(mesh):
    in_specs = (P("vel", "cell", None), P("cell", None), P())
    out_specs = (P("vel", "cell", None), P(None, "cell", None))
    body = functools.partial(shards, 4, 8)
    return jax.shard_map(body, mesh=mesh, in_specs=in_specs, out_specs=out_specs, check_vma=False)
```

```python
import functools

import jax
import jax.numpy as jnp
import numpy as np
from jax import lax
from jax.experimental import pallas as pl
from jax.experimental.pallas import tpu as pltpu
from jax.sharding import PartitionSpec as P

QUAD_ABSCISSAE = 24
RUN = 6
STEPS = 2


MOMENTUM_RATIO = 2.0 / 3.0
SHEAR_EXPONENT = 0.81
SHEAR_REFERENCE = 0.05
TIME_INCREMENT = 0.03125

NODES = RUN * RUN * RUN
HALF = NODES // 2
EARLY = 80
PAIRS = RUN * RUN
USED = 26
ROWS = 32
ORDER = (4, 3, 5, 2, 6, 1, 7)
MESH = pl.DeviceIdType.MESH


def hermite_rule(points):
    start_value = np.pi ** (-0.25)
    node_list = np.zeros(points)
    weight_list = np.zeros(points)
    guess_root = 0.0
    slope_value = 1.0
    for index in range((points + 1) // 2):
        if index == 0:
            guess_root = np.sqrt(2.0 * points + 1.0) - 1.85575 * (2.0 * points + 1.0) ** (-0.16667)
        elif index == 1:
            guess_root = guess_root - 1.14 * points**0.426 / guess_root
        elif index == 2:
            guess_root = 1.86 * guess_root - 0.86 * node_list[0]
        elif index == 3:
            guess_root = 1.91 * guess_root - 0.91 * node_list[1]
        else:
            guess_root = 2.0 * guess_root - node_list[index - 2]
        for sweep in range(60):
            poly_now = start_value
            poly_prev = 0.0
            for degree in range(points):
                poly_old = poly_prev
                poly_prev = poly_now
                poly_now = (
                    guess_root * np.sqrt(2.0 / (degree + 1)) * poly_prev
                    - np.sqrt(degree / (degree + 1.0)) * poly_old
                )
            slope_value = np.sqrt(2.0 * points) * poly_prev
            guess_root = guess_root - poly_now / slope_value
        node_list[index] = guess_root
        node_list[points - 1 - index] = -guess_root
        weight_list[index] = 2.0 / (slope_value * slope_value)
        weight_list[points - 1 - index] = weight_list[index]
    return (node_list[::-1].copy(), weight_list[::-1].copy())


def one_dimensional_tables(points):
    abscissa, weights = hermite_rule(points)
    speed = np.sqrt(2.0) * abscissa
    weight = weights * np.exp(abscissa * abscissa) / np.sqrt(np.pi)
    return np.concatenate([speed, weight, TIME_INCREMENT * np.abs(speed)])


def step_parameters(moment, kind, boundary):
    density = moment[0]
    first = moment[1:4]
    flow = [value / density for value in first]
    trace = moment[4] + moment[5] + moment[6]
    square = flow[0] * flow[0] + flow[1] * flow[1] + flow[2] * flow[2]
    temperature = (trace / density - square) / 3.0
    along = flow[0] * first[0] + flow[1] * first[1] + flow[2] * first[2]
    pairs = ((4, 7, 8), (7, 5, 9), (8, 9, 6))
    heat = []
    for d in range(3):
        tensor = (
            moment[pairs[d][0]] * flow[0]
            + moment[pairs[d][1]] * flow[1]
            + moment[pairs[d][2]] * flow[2]
        )
        heat.append(
            0.5
            * (
                moment[10 + d]
                - 2.0 * tensor
                + square * first[d]
                - flow[d] * trace
                + 2.0 * flow[d] * along
                - flow[d] * square * density
            )
        )
    pressure = density * temperature
    rate = (
        TIME_INCREMENT
        * pressure
        / (SHEAR_REFERENCE * jnp.exp(SHEAR_EXPONENT * jnp.log(temperature)))
    )
    keep = 1.0 / (1.0 + rate)
    scale = (1.0 - MOMENTUM_RATIO) / (5.0 * pressure * temperature)

    def pick(fluid, wall, inlet, outlet):
        return jnp.where(
            kind == 0, fluid, jnp.where(kind == 1, wall, jnp.where(kind == 2, inlet, outlet))
        )

    level = pick(temperature, boundary[5], boundary[4], 1.0)
    amount = pick(density * rate * keep, density, boundary[0], 0.0)
    return (
        [pick(keep, 0.0, 0.0, 1.0), amount / (level * jnp.sqrt(level))]
        + [pick(flow[d], 0.0, boundary[1 + d], 0.0) for d in range(3)]
        + [0.5 / level]
        + [pick(heat[d] * scale, 0.0, 0.0, 0.0) for d in range(3)]
        + [density, first[0], first[1], first[2], trace]
    )


def added_moments(power, amount, flow, inverse, heat):
    planes = {}

    def product(i, j, k):
        if (i, j) not in planes:
            planes[i, j] = power[0][i] * power[1][j]
        return planes[i, j] * power[2][k]

    def shifted(base, d, n=1):
        return tuple(base[e] + (n if e == d else 0) for e in range(3))

    def squared(base):
        return product(*shifted(base, 0, 2)) + product(*shifted(base, 1, 2)) + product(*shifted(base, 2, 2))

    double = inverse + inverse

    def whole(base):
        total = product(*base)
        for d in range(3):
            with_d = shifted(base, d)
            total = total + heat[d] * (double * squared(with_d) - 5.0 * product(*with_d))
        return total

    def with_heat(base, d):
        at = shifted(base, d)
        fourth = None
        for e in range(3):
            for f in range(3):
                term = product(*shifted(shifted(at, e, 2), f, 2))
                fourth = term if fourth is None else fourth + term
        return heat[d] * (double * fourth - 5.0 * squared(at))

    zero = (0, 0, 0)
    none = amount * whole(zero)
    one = [amount * whole(shifted(zero, d)) for d in range(3)]
    two = squared(zero)
    for d in range(3):
        two = two + with_heat(zero, d)
    two = amount * two
    square = flow[0] * flow[0] + flow[1] * flow[1] + flow[2] * flow[2]
    momentum = [one[d] + flow[d] * none for d in range(3)]
    trace = (
        two
        + 2.0 * (flow[0] * one[0] + flow[1] * one[1] + flow[2] * one[2])
        + square * none
    )
    return [none] + momentum + [trace]


def kernel(
    digits,
    cells,
    state_ref,
    kind_hbm,
    boundary_ref,
    out_ref,
    macro_ref,
    kind_ref,
    table_ref,
    raw,
    h_first,
    h_second,
    moved,
    halo,
    acc,
    edge,
    edge_part,
    got_edge,
    edge_sum,
    part,
    got_a,
    mine,
    got_b,
    gathered,
    gauss,
    bend,
    tilt,
    keep_ref,
    input_sem,
    send_sem,
    recv_sem,
    edge_send,
    edge_recv,
    halo_send,
    halo_recv,
):
    points = RUN * digits
    vel = lax.axis_index("vel")
    cell = lax.axis_index("cell")
    jc = lax.rem(vel, digits)
    jb = lax.rem(vel // digits, digits)
    ja = vel // (digits * digits)
    lo = lax.rem(vel, 2)
    row = lax.rem(vel // 2, 8)
    col = vel // 16
    here = col * 2 + lax.rem(row, 2)
    there = (row // 2) * 2 + lo
    up = lax.rem(cell + 1, cells)
    down = lax.rem(cell + cells - 1, cells)

    def peer_a(other, slab):
        return ((other // 2) * 16 + (row // 2 * 2 + lax.rem(other, 2)) * 2 + lo, slab)

    def peer_b(other, slab):
        return (col * 16 + (other // 2 * 2 + lax.rem(row, 2)) * 2 + lax.rem(other, 2), slab)

    loads = [
        pltpu.make_async_copy(state_ref, raw, input_sem.at[0]),
        pltpu.make_async_copy(kind_hbm, kind_ref, input_sem.at[1]),
    ]
    barrier = pltpu.get_barrier_semaphore()
    greeted = [peer_a(lax.rem(here + k, 8), other) for k in range(8) for other in (up, down)]
    greeted += [peer_a(lax.rem(here + k, 8), cell) for k in range(1, 8)]
    greeted += [peer_b(lax.rem(there + k, 8), cell) for k in range(1, 8)]
    for device in greeted:
        pl.semaphore_signal(barrier, inc=1, device_id=device, device_id_type=MESH)
    for copy in loads:
        copy.start()
    for index, value in enumerate(one_dimensional_tables(points)):
        table_ref[index] = jnp.float32(value)

    lane = lax.broadcasted_iota(jnp.int32, (8, 128), 1)
    sub = lax.broadcasted_iota(jnp.int32, (8, 128), 0)
    in_z = lax.rem(lane, 32)
    z_first, z_last = in_z == 0, in_z == 31
    y_low, y_high = lane < 32, lane >= 96
    y_first, y_last = sub == 0, sub == 7
    has_down = jnp.where(cell > 0, 1.0, 0.0).astype(jnp.float32)
    has_up = jnp.where(cell < cells - 1, 1.0, 0.0).astype(jnp.float32)

    def speed(m, digit):
        return table_ref[4 * m + digit] if digits == 4 else table_ref[m]

    def weight(m, digit):
        return table_ref[points + 4 * m + digit] if digits == 4 else table_ref[points + m]

    def courant(m, digit):
        return table_ref[2 * points + 4 * m + digit] if digits == 4 else table_ref[2 * points + m]

    def run_sums(values):
        sums = None
        for mc, value in enumerate(values):
            sz = speed(mc, jc)
            terms = [weight(mc, jc) * value]
            for _ in range(3):
                terms.append(sz * terms[-1])
            sums = terms if sums is None else [x + y for x, y in zip(sums, terms)]
        return sums

    def add_run(total, values, mb):
        sy, w = speed(mb, jb), weight(mb, jb)
        result = []
        for n, term in enumerate(run_sums(values)):
            term = w * term
            row = [term]
            for _ in range(3 - n):
                term = sy * term
                row.append(term)
            if total is not None:
                row = [x + y for x, y in zip(total[n], row)]
            result.append(row)
        return result

    def add_moments(ref, place, total, ma, factor):
        sx = speed(ma, ja)
        w = weight(ma, ja) * factor
        wx, square = w * sx, sx * sx
        (z0, z0y, z0yy, z0yyy), (z1, z1y, z1yy), (z2, z2y), (z3,) = total
        rows = [
            w * z0,
            wx * z0,
            w * z0y,
            w * z1,
            (wx * sx) * z0,
            w * z0yy,
            w * z2,
            wx * z0y,
            wx * z1,
            w * z1y,
            wx * (square * z0 + (z0yy + z2)),
            w * (square * z0y + (z0yyy + z2y)),
            w * (square * z1 + (z1yy + z3)),
        ]
        for r in range(13):
            ref[r, place] += rows[r]

    def shift_y(value, positive):
        turned = pltpu.roll(value, 32 if positive else 96, 1)
        carried = pltpu.roll(turned, 1 if positive else 7, 0)
        edge_rows, lanes = (y_first, y_low) if positive else (y_last, y_high)
        return jnp.where(lanes, jnp.where(edge_rows, 0.0, carried), turned)

    def shift_z(value, positive):
        turned = pltpu.roll(value, 1 if positive else 127, 1)
        return jnp.where(z_first if positive else z_last, 0.0, turned)

    def relaxed(i, ma, mb, plane, pi, outer):
        base = gauss[ma, plane] * gauss[RUN + mb, plane]
        bend_xy = bend[ma, plane] + bend[RUN + mb, plane]
        tilt_xy = tilt[ma, plane] + tilt[RUN + mb, plane]
        keep = keep_ref[plane]
        values = []
        if outer:
            kx = courant(ma, ja) * jnp.where(pi == 1, has_down, has_up)
        for mc in range(RUN):
            node = i * RUN + mc
            value = moved[plane, node]
            if outer:
                value = value + kx * halo[outer - 1, pi, node - pi * HALF]
            t = (tilt_xy + tilt[2 * RUN + mc, plane]) * (bend_xy + bend[2 * RUN + mc, plane])
            values.append(keep * value + (base * gauss[2 * RUN + mc, plane]) * (1.0 + t))
        return values

    def new_plane(step, i, ma, mb, plane, pi, outer):
        if step == 0:
            return [
                raw[pl.ds((i * RUN + mc) * 16 + plane, 8, stride=2), :] for mc in range(RUN)
            ]
        return relaxed(i, ma, mb, plane, pi, step if outer else 0)

    def send_edges(step, held):
        copies = []
        for r in range(13):
            for pi in range(2):
                edge_part[step, pi, pl.ds(r, 8, stride=16), :] = edge[pi, r]
        for k in ORDER + (0,):
            other = lax.rem(here + k, 8)
            for pi, slab in ((1, up), (0, down)):
                copies.append(
                    pltpu.make_async_remote_copy(
                        src_ref=edge_part.at[step, pi, pl.ds(pl.multiple_of(other * 16, 16), 13)],
                        dst_ref=got_edge.at[step, pi, here],
                        send_sem=edge_send.at[step, pi, k],
                        recv_sem=edge_recv.at[step, pi, k],
                        device_id=peer_a(other, slab),
                        device_id_type=MESH,
                    )
                )
        for part_index, (first, count) in enumerate(((0, EARLY), (EARLY, HALF - EARLY))):
            for pi, other in ((1, up), (0, down)):
                copies.append(
                    pltpu.make_async_remote_copy(
                        src_ref=held.at[pl.ds(pi * HALF + first, count)],
                        dst_ref=halo.at[step, pi, pl.ds(first, count)],
                        send_sem=halo_send.at[step, part_index, pi],
                        recv_sem=halo_recv.at[step, part_index, pi],
                        device_id=(vel, other),
                        device_id_type=MESH,
                    )
                )
        for copy in copies[:18]:
            copy.start()
        return copies[:16], copies[16:]

    def exchange(step, phase, source, target, index, peer):
        copies = []
        for k in ORDER:
            other = lax.rem(index + k, 8)
            copy = pltpu.make_async_remote_copy(
                src_ref=source(other),
                dst_ref=target,
                send_sem=send_sem.at[step, phase, k - 1],
                recv_sem=recv_sem.at[step, phase, k - 1],
                device_id=peer(other, cell),
                device_id_type=MESH,
            )
            copy.start()
            copies.append(copy)
        return copies

    def slice_rows(index, count):
        return pl.ds(pl.multiple_of(index * ROWS, ROWS), count)

    def parameters_of(step, index, total_ref):
        moment = [total_ref[pl.ds(r, 2, stride=13), :] for r in range(13)]
        kind = kind_ref[pl.ds(2 * index, 2), :]
        boundary = [boundary_ref[r] for r in range(6)]
        rows = step_parameters(moment, kind, boundary)
        for r in range(9 if step < STEPS - 1 else 14):
            gathered[step, pl.ds(index * ROWS + 2 * r, 2), :] = rows[r]

    def all_sums(step, edges, late):
        for r in range(13):
            for p in range(2):
                part[step, pl.ds(13 * p + r, 8, stride=ROWS), :] = acc[r, p]
        copies = exchange(
            step, 0, lambda other: part.at[step, slice_rows(other, USED)], got_a.at[step, here], here, peer_a
        )
        got_a[step, here] = part[step, slice_rows(here, USED), :]
        for copy in edges:
            copy.wait()
        for p in range(2):
            from_edge = got_edge[step, 1 - p, 0]
            for k in range(1, 8):
                from_edge = from_edge + got_edge[step, 1 - p, k]
            edge_sum[pl.ds(13 * p, 13), :] = from_edge * (has_down if p == 0 else has_up)
        for copy in copies:
            copy.wait()
        total = edge_sum[...]
        for k in range(8):
            total = total + got_a[step, k]
        mine[step] = total
        copies = exchange(
            step, 1, lambda other: mine.at[step], got_b.at[step, there], there, peer_b
        )
        got_b[step, there] = total
        for copy in copies:
            copy.wait()
        for copy in late:
            copy.start()
        total = got_b[step, 0]
        for k in range(1, 8):
            total = total + got_b[step, k]
        acc_rows = got_b.at[step, there]
        acc_rows[...] = total
        parameters_of(step, here, acc_rows)
        block = gathered.at[step, slice_rows(here, 18 if step < STEPS - 1 else 28)]
        copies = exchange(step, 2, lambda other: block, block, here, peer_a)
        for copy in copies:
            copy.wait()

    def gathered_rows(step, r):
        return [gathered[step, pl.ds(2 * r + p, 8, stride=ROWS), :] for p in range(2)]

    def build_tables(step):
        keep, amount, *rest = [gathered_rows(step, r) for r in range(9)]
        for p in range(2):
            keep_ref[p] = keep[p]

        def fill(m, carry):
            for d, digit in enumerate((ja, jb, jc)):
                s = speed(m, digit)
                for p in range(2):
                    c = s - rest[d][p]
                    inverse = rest[3][p]
                    scaled = c * c * inverse
                    value = jnp.exp(-scaled)
                    lift = scaled + scaled
                    if d == 0:
                        value = value * amount[p]
                        lift = lift - 5.0
                    gauss[d * RUN + m, p] = value
                    bend[d * RUN + m, p] = lift
                    tilt[d * RUN + m, p] = c * rest[4 + d][p]
            return carry

        lax.fori_loop(0, RUN, fill, 0)

    for copy in loads:
        copy.wait()
    for step in range(STEPS):
        held = h_first if step == 0 else h_second
        edge[...] = jnp.zeros(edge.shape, jnp.float32)
        acc[...] = jnp.zeros(acc.shape, jnp.float32)

        def inner(ma, carry, step=step, held=held):
            pi = ma // (RUN // 2)
            total = None
            for mb in range(RUN):
                i = ma * RUN + mb
                values = new_plane(step, i, ma, mb, pi, pi, False)
                for mc in range(RUN):
                    held[i * RUN + mc] = values[mc]
                total = add_run(total, values, mb)
            add_moments(edge.at[pi], slice(None), total, ma, courant(ma, ja))
            return carry

        lax.fori_loop(0, RUN, inner, 0)
        if step == 0:
            pl.semaphore_wait(barrier, len(greeted))
        edges, halos = send_edges(step, held)
        if step > 0:
            for copy in halos_before:
                copy.wait()

        for half in range(2):

            def transport(ma, carry, half=half, step=step, held=held):
                pi = ma // (RUN // 2)
                kx = courant(ma, ja)
                inner_total, outer_total = None, None
                for mb in range(half * (RUN // 2), (half + 1) * (RUN // 2)):
                    i = ma * RUN + mb
                    ky = courant(mb, jb)
                    at_inner, at_outer = [], []
                    values = new_plane(step, i, ma, mb, 1 - pi, pi, True)
                    for mc in range(RUN):
                        node = i * RUN + mc
                        kz = courant(mc, jc)
                        stay = 1.0 - (kx + ky + kz)
                        near, far = held[node], values[mc]

                        def flat(value):
                            return (
                                stay * value
                                + ky * shift_y(value, half == 1)
                                + kz * shift_z(value, mc >= RUN // 2)
                            )

                        at_inner.append(flat(near) + kx * far)
                        at_outer.append(flat(far))
                        moved[pi, node] = at_inner[-1]
                        moved[1 - pi, node] = at_outer[-1]
                    inner_total = add_run(inner_total, at_inner, mb)
                    outer_total = add_run(outer_total, at_outer, mb)
                add_moments(acc, pi, inner_total, ma, 1.0)
                add_moments(acc, 1 - pi, outer_total, ma, 1.0)
                return carry

            lax.fori_loop(0, RUN, transport, 0, unroll=2)
        all_sums(step, edges, halos[2:])
        build_tables(step)
        halos_before = halos

    final = STEPS - 1
    for p in range(2):
        keep, amount, ux, uy, uz, inverse, qx, qy, qz, *old = [
            gathered_rows(final, r)[p] for r in range(14)
        ]
        flow, heat = (ux, uy, uz), (qx, qy, qz)

        def sums(a, carry):
            s, w = table_ref[a], table_ref[points + a]
            result = []
            for d in range(3):
                c = s - flow[d]
                term = w * jnp.exp(-(c * c * inverse))
                for n in range(6):
                    result.append(carry[d * 6 + n] + term)
                    term = term * c
            return tuple(result)

        power = lax.fori_loop(
            0, points, sums, tuple(jnp.zeros((8, 128), jnp.float32) for _ in range(18)), unroll=4
        )
        power = [power[d * 6 : d * 6 + 6] for d in range(3)]
        added = added_moments(power, amount, flow, inverse, heat)
        density, mx, my, mz, trace = [keep * x + y for x, y in zip(old, added)]
        u = [mx / density, my / density, mz / density]
        square = u[0] * u[0] + u[1] * u[1] + u[2] * u[2]
        result = [density] + u + [(trace / density - square) / 3.0]
        for r in range(5):
            macro_ref[pl.ds(r * 16 + p, 8, stride=2), :] = result[r]

    def last(is_outer):
        def body(i, carry):
            ma, mb = i // RUN, lax.rem(i, RUN)
            pi = ma // (RUN // 2)
            plane = 1 - pi if is_outer else pi
            values = relaxed(i, ma, mb, plane, pi, STEPS if is_outer else 0)
            for mc in range(RUN):
                out_ref[pl.ds((i * RUN + mc) * 16 + plane, 8, stride=2), :] = values[mc]
            return carry

        lax.fori_loop(0, PAIRS, body, 0, unroll=3)

    last(False)
    for copy in halos_before:
        copy.wait()
    last(True)


def interleaved(array):
    lead = array.shape[:-2]
    return array.reshape(lead + (2, 8, 128)).swapaxes(-3, -2).reshape(-1, 128)


def restored(array, lead):
    return array.reshape((lead, 8, 2, 128)).swapaxes(1, 2).reshape(lead, 2, 1024)


def shards(digits, cells, state_init, cell_kind, boundary_state):
    vmem = functools.partial(pl.BlockSpec, memory_space=pltpu.VMEM)
    smem = functools.partial(pl.BlockSpec, memory_space=pltpu.SMEM)
    f32 = jnp.float32
    state, macro = pl.pallas_call(
        functools.partial(kernel, digits, cells),
        out_shape=(
            jax.ShapeDtypeStruct((NODES * 16, 128), f32),
            jax.ShapeDtypeStruct((80, 128), f32),
        ),
        in_specs=[pl.BlockSpec(memory_space=pltpu.HBM), pl.BlockSpec(memory_space=pltpu.HBM), smem()],
        out_specs=(vmem(), vmem()),
        scratch_shapes=[
            pltpu.VMEM((16, 128), jnp.int32),
            pltpu.SMEM((3 * RUN * digits,), f32),
            pltpu.VMEM((NODES * 16, 128), f32),
            pltpu.VMEM((NODES, 8, 128), f32),
            pltpu.VMEM((NODES, 8, 128), f32),
            pltpu.VMEM((2, NODES, 8, 128), f32),
            pltpu.VMEM((STEPS, 2, HALF, 8, 128), f32),
            pltpu.VMEM((13, 2, 8, 128), f32),
            pltpu.VMEM((2, 13, 8, 128), f32),
            pltpu.VMEM((STEPS, 2, 8 * 16, 128), f32),
            pltpu.VMEM((STEPS, 2, 8, 13, 128), f32),
            pltpu.VMEM((USED, 128), f32),
            pltpu.VMEM((STEPS, 8 * ROWS, 128), f32),
            pltpu.VMEM((STEPS, 8, USED, 128), f32),
            pltpu.VMEM((STEPS, USED, 128), f32),
            pltpu.VMEM((STEPS, 8, USED, 128), f32),
            pltpu.VMEM((STEPS, 8 * ROWS, 128), f32),
            pltpu.VMEM((3 * RUN, 2, 8, 128), f32),
            pltpu.VMEM((3 * RUN, 2, 8, 128), f32),
            pltpu.VMEM((3 * RUN, 2, 8, 128), f32),
            pltpu.VMEM((2, 8, 128), f32),
            pltpu.SemaphoreType.DMA((2,)),
            pltpu.SemaphoreType.DMA((STEPS, 3, 7)),
            pltpu.SemaphoreType.DMA((STEPS, 3, 7)),
            pltpu.SemaphoreType.DMA((STEPS, 2, 8)),
            pltpu.SemaphoreType.DMA((STEPS, 2, 8)),
            pltpu.SemaphoreType.DMA((STEPS, 2, 2)),
            pltpu.SemaphoreType.DMA((STEPS, 2, 2)),
        ],
        compiler_params=pltpu.CompilerParams(
            collective_id=0, has_side_effects=True, vmem_limit_bytes=52 * 1024 * 1024
        ),
    )(interleaved(state_init), interleaved(cell_kind), boundary_state)
    return restored(state, NODES), restored(macro, 5)


def solution(mesh):
    in_specs = (P("vel", "cell", None), P("cell", None), P())
    out_specs = (P("vel", "cell", None), P(None, "cell", None))
    body = functools.partial(shards, 4, 8)
    return jax.shard_map(body, mesh=mesh, in_specs=in_specs, out_specs=out_specs, check_vma=False)
```
